256 devices in a mesh: row: 16 (over z_lo, y, core), col: 16 (over x, z_hi).
Axes of the slice: x: 4, y: 4, z: 8 (z_hi: 4, z_lo: 2; z = z_hi * 2 + z_lo), core: 2. Of those that a mesh axis runs over, the one named last changes fastest.
Arguments:
- features: bfloat16 [65536, 128], P(('col', 'row')), may hold values from -6 to 6
- weight: bfloat16 [128, 256], replicated, may hold values from -0.5 to 0.5
- bias: float32 [256], replicated, may hold values from -3 to 3
- cotangent: bfloat16 [65536, 256], P(('row', 'col')), may hold values from -6 to 6
- tile_rows: int32 [16, 16, 160], P('row', 'col'), may hold values from 0 to 31
- tile_cols: int32 [16, 16, 160], P('row', 'col'), may hold values from 0 to 31
- tile_mask: int32 [16, 16, 160, 128, 128], P('row', 'col'), may hold values from 0 to 1, as said below
Outputs:
- activations: bfloat16 [65536, 256], P(('row', 'col'))
- grad_features: bfloat16 [65536, 128], P(('col', 'row'))
- grad_weight: float32 [128, 256], replicated
- grad_bias: float32 [256], replicated
The draws below stay inside these ranges and needn't reach their ends.
Inputs may be any that keep to these rules, and one draw needn't show every extreme that they name: `tile_mask`: entries are 0 or 1. On each device the slots that hold any entry come first; every such slot has its entry at a = b = 0 set; in every grid row one device has all 160 slots holding entries.
All inputs are finite; a program needn't handle non-finite values.
Results may differ from the reference program's by a relative error of at most 0.0049.
Values may be sent and summed in bfloat16 or wider, within the bound.
A program may use at most 128 MiB of HBM per device.

```python
import jax
import jax.numpy as jnp
from jax import lax

F_IN = 128
HID = 256
TILES_DEV = 160
TBR = 32
TBC = 32
NODES = 65536
N_ROW = 16
N_COL = 16


def draw_tile_mask(key, part):
    key = jax.random.fold_in(key, 11)
    live_key, entry_key = jax.random.split(key)
    shape = (N_ROW, N_COL, TILES_DEV, 128, 128)
    row_pos = jnp.arange(N_ROW, dtype=jnp.int32)[:, None, None, None, None]
    col_pos = jnp.arange(N_COL, dtype=jnp.int32)[None, :, None, None, None]
    slot_pos = jnp.arange(TILES_DEV, dtype=jnp.int32)[None, None, :, None, None]
    home_col = row_pos * N_COL // N_ROW
    live_other = jax.random.randint(live_key, (N_ROW, N_COL, 1, 1, 1), max(1, TILES_DEV // 8), max(1, TILES_DEV // 2) + 1)
    live_count = jnp.where(col_pos == home_col, TILES_DEV, live_other)
    row_base = max(N_ROW - 1, 1)
    col_base = max(N_COL - 1, 1)
    level = (row_base + 2 * row_pos) * (col_base + 2 * col_pos)
    drawn = jax.random.randint(entry_key, shape, 0, 250 * row_base * col_base)
    inner_a = jnp.arange(128, dtype=jnp.int32)[:, None]
    inner_b = jnp.arange(128, dtype=jnp.int32)[None, :]
    corner = (inner_a == 0) & (inner_b == 0)
    present = ((drawn < level) | corner) & (slot_pos < live_count)
    return present.astype(jnp.int32)


def touch_ends(values, key, smallest, high):
    longest = values.shape.index(max(values.shape))
    spots = []
    for shift in (0, 1):
        where = [jax.random.randint(jax.random.fold_in(key, axis), (), 0, length) for axis, length in enumerate(values.shape)]
        where[longest] = (where[longest] + shift) % values.shape[longest]
        spots.append(tuple(where))
    return values.at[spots[0]].set(smallest).at[spots[1]].set(high)


def block_levels(key, extent, pieces, least, high):
    def one(axis_at, parts):
        draws = jax.random.uniform(jax.random.fold_in(jax.random.fold_in(key, 6), axis_at), (parts,), jnp.float32, least / len(pieces), high / len(pieces))
        return jnp.repeat(jnp.exp(draws), extent[axis_at] // parts).reshape((-1,) + (1,) * (len(extent) - axis_at - 1))

    gain = one(*pieces[0])
    for cut in pieces[1:]:
        gain = gain * one(*cut)
    return gain


def noise(key, dims, spread, bound, cuts=(), held_as=jnp.bfloat16):
    factor_of = block_levels(key, dims, cuts, -0.22, 0.18) if cuts else 1.0
    values = jax.random.normal(key, dims, jnp.float32) * spread * factor_of
    return jnp.minimum(jnp.maximum(values, -bound), bound).astype(held_as)


def setup_inputs(seed: int = 0) -> dict:
    key_of = jax.random.split(jax.random.key(seed), 8)
    features = noise(key_of[0], (NODES, F_IN), 1.0, 6.0, ((0, 256),))
    weight = noise(key_of[1], (F_IN, HID), F_IN ** -0.5, 0.5)
    bias = noise(key_of[2], (HID,), 0.5, 3.0, (), jnp.float32)
    cotangent = noise(key_of[3], (NODES, HID), 1.0, 6.0, ((0, 256),))
    tile_rows = touch_ends(jax.random.randint(key_of[4], (N_ROW, N_COL, TILES_DEV), 0, TBR), jax.random.fold_in(key_of[4], 1), 0, TBR - 1).astype(jnp.int32)
    tile_cols = touch_ends(jax.random.randint(key_of[5], (N_ROW, N_COL, TILES_DEV), 0, TBC), jax.random.fold_in(key_of[5], 1), 0, TBC - 1).astype(jnp.int32)
    tile_mask = draw_tile_mask(jax.random.fold_in(key_of[7], 71), 0)
    return dict(features=features, weight=weight, bias=bias, cotangent=cotangent, tile_rows=tile_rows, tile_cols=tile_cols, tile_mask=tile_mask)


def select_rows(tile_ids, count):
    return (tile_ids[:, None] == jnp.arange(count, dtype=jnp.int32)[None, :]).astype(jnp.float32)

def tiles_forward(entries, row_ids, col_ids, source, row_tiles):
    width = source.shape[1]
    picked = source.reshape(-1, 128, width)[col_ids].astype(jnp.float32)
    products = jnp.einsum('sab,sbh->sah', entries.astype(jnp.float32), picked, precision=lax.Precision.HIGHEST)
    placed = jnp.einsum('st,sah->tah', select_rows(row_ids, row_tiles), products, precision=lax.Precision.HIGHEST)
    return placed.reshape(row_tiles * 128, width)

def tiles_backward(entries, row_ids, col_ids, source, col_tiles):
    width = source.shape[1]
    picked = source.reshape(-1, 128, width)[row_ids].astype(jnp.float32)
    products = jnp.einsum('sab,sah->sbh', entries.astype(jnp.float32), picked)
    placed = jnp.einsum('st,sbh->tbh', select_rows(col_ids, col_tiles), products, precision=lax.Precision.HIGHEST)
    return placed.reshape(col_tiles * 128, width)

def reference(features, weight, bias, cotangent, tile_rows, tile_cols, tile_mask):
    grid_rows, grid_cols, slot_count = tile_rows.shape
    nodes = features.shape[0]
    hidden = weight.shape[1]
    inputs = weight.shape[0]
    row_span = nodes // grid_rows
    col_span = nodes // grid_cols
    row_tiles = row_span // 128
    col_tiles = col_span // 128

    def device_counts(index):
        row_pos = index // grid_cols
        col_pos = index % grid_cols
        entries = tile_mask[row_pos, col_pos].astype(jnp.float32)
        by_rows = jnp.einsum('st,sa->ta', select_rows(tile_rows[row_pos, col_pos], row_tiles), lax.optimization_barrier(jnp.sum(entries, axis=2)), precision=lax.Precision.HIGHEST)
        by_cols = jnp.einsum('st,sb->tb', select_rows(tile_cols[row_pos, col_pos], col_tiles), lax.optimization_barrier(jnp.sum(entries, axis=1)), precision=lax.Precision.HIGHEST)
        return (by_rows.reshape(row_span), by_cols.reshape(col_span))
    row_parts, col_parts = lax.map(device_counts, jnp.arange(grid_rows * grid_cols, dtype=jnp.int32))
    row_count = lax.optimization_barrier(jnp.sum(row_parts.reshape(grid_rows, grid_cols, row_span), axis=1)).reshape(nodes)
    col_count = lax.optimization_barrier(jnp.sum(col_parts.reshape(grid_rows, grid_cols, col_span), axis=0)).reshape(nodes)
    row_scale = 1.0 / jnp.sqrt(1.0 + row_count)
    col_scale = 1.0 / jnp.sqrt(1.0 + col_count)
    scaled = features.astype(jnp.float32) * col_scale[:, None]

    def forward_block(row_pos):

        def add_col(col_pos, total):
            source = lax.dynamic_slice_in_dim(scaled, (col_pos * col_span).astype(jnp.int32), col_span, 0)
            return total + tiles_forward(tile_mask[row_pos, col_pos], tile_rows[row_pos, col_pos], tile_cols[row_pos, col_pos], source, row_tiles)
        return lax.fori_loop(0, grid_cols, add_col, jnp.zeros((row_span, inputs), jnp.float32))
    aggregated = lax.map(forward_block, jnp.arange(grid_rows, dtype=jnp.int32)).reshape(nodes, inputs)
    weight_wide = weight.astype(jnp.float32)
    summed = jnp.dot(aggregated, weight_wide, precision=lax.Precision.HIGHEST)
    pre_act = row_scale[:, None] * summed + bias[None, :]
    sigmoid_z = jax.nn.sigmoid(pre_act)
    activations = (pre_act * sigmoid_z).astype(jnp.bfloat16)
    grad_pre = cotangent.astype(jnp.float32) * sigmoid_z * (1.0 + pre_act * (1.0 - sigmoid_z))
    sent = (row_scale[:, None] * grad_pre).astype(jnp.bfloat16)

    def backward_block(col_pos):

        def add_row(row_pos, total):
            source = lax.dynamic_slice_in_dim(sent, (row_pos * row_span).astype(jnp.int32), row_span, 0)
            return total + tiles_backward(tile_mask[row_pos, col_pos], tile_rows[row_pos, col_pos], tile_cols[row_pos, col_pos], source, col_tiles)
        return lax.fori_loop(0, grid_rows, add_row, jnp.zeros((col_span, hidden), jnp.float32))
    back_sum = lax.map(backward_block, jnp.arange(grid_cols, dtype=jnp.int32)).reshape(nodes, hidden)
    column_grad = col_scale[:, None] * back_sum
    grad_features = jnp.dot(column_grad, weight_wide.T, precision=lax.Precision.HIGHEST).astype(jnp.bfloat16)
    factor = 1.0 / jnp.sqrt(jnp.float32(nodes))
    grad_weight = jnp.dot(features.astype(jnp.float32).T, column_grad, precision=lax.Precision.HIGHEST) * factor
    grad_bias = lax.optimization_barrier(jnp.sum(grad_pre, axis=0)) * factor
    return (activations, grad_features, grad_weight, grad_bias)
```

```python
import functools

import jax
import jax.numpy as jnp
from jax import lax
from jax.experimental import pallas as pl
from jax.experimental.pallas import tpu as pltpu
from jax.sharding import PartitionSpec as P

F32 = jnp.float32
BF16 = jnp.bfloat16
T = 128
SLOTS = 160
CHUNK = 16
VMEM_LIMIT = 40 * 1024 * 1024
ROW_STEPS = tuple((dz, dy) for dz in range(2) for dy in range(4) if (dz, dy) != (0, 0))


def send(src, dst, send_sem, recv_sem, row, col):
    return pltpu.make_async_remote_copy(
        src_ref=src,
        dst_ref=dst,
        send_sem=send_sem,
        recv_sem=recv_sem,
        device_id=(row, col),
        device_id_type=pl.DeviceIdType.MESH,
    )


def row_place():
    row = lax.axis_index("row")
    return row // 8, (row // 2) % 4, row % 2


def row_at(zl, y, core):
    return zl * 8 + y * 2 + core


def greet(devices):
    barrier = pltpu.get_barrier_semaphore()
    for row, col in devices:
        pl.semaphore_signal(
            barrier, inc=1, device_id=(row, col), device_id_type=pl.DeviceIdType.MESH
        )
    pl.semaphore_wait(barrier, len(devices))


def split_dot(a, b):
    hi = a.astype(BF16)
    lo = (a - hi.astype(F32)).astype(BF16)
    return jnp.dot(hi, b, preferred_element_type=F32) + jnp.dot(lo, b, preferred_element_type=F32)


def spread_kernel(
    feat, col_ids, mask, narrow_out, scaled_out, scale_out,
    mask_in, narrow, feats, sums, count, sib_count, pair, far_count,
    mask_sem, narrow_sem, f_send, f_recv, g_send, g_recv, c_send, c_recv,
):
    row, col = lax.axis_index("row"), lax.axis_index("col")
    zl, y, core = row_place()
    sibling = row_at(zl, y, 1 - core)
    to = [row_at((zl + dz) % 2, (y + dy) % 4, core) for dz, dy in ROW_STEPS]
    frm = [row_at((zl - dz + 2) % 2, (y - dy + 4) % 4, core) for dz, dy in ROW_STEPS]
    n = len(ROW_STEPS)
    chunks = SLOTS // CHUNK
    loads = []
    for c in range(chunks):
        span = pl.ds(c * CHUNK, CHUNK)
        load = pltpu.make_async_copy(mask.at[span], mask_in.at[span], mask_sem.at[c])
        load.start()
        loads.append(load)
    greet([(sibling, col)] + [(p, col) for p in to])
    own = [send(feat, feats.at[row], f_send.at[k], f_recv.at[k], to[k], col) for k in range(n)]
    own.append(send(feat, feats.at[row], f_send.at[n], f_recv.at[n], sibling, col))
    for copy in own:
        copy.start()
    feats[row] = feat[...]
    stores = []
    for c in range(chunks):
        loads[c].wait()

        def eight(g, carry):
            at = pl.multiple_of(c * CHUNK + g * 8, 8)
            wide = mask_in[pl.ds(at, 8)].astype(F32)
            narrow[pl.ds(at, 8)] = wide.astype(BF16)
            sums[pl.ds(at, 8), :] = jnp.sum(wide, axis=1)
            return carry

        lax.fori_loop(0, CHUNK // 8, eight, 0)
        span = pl.ds(c * CHUNK, CHUNK)
        store = pltpu.make_async_copy(narrow.at[span], narrow_out.at[span], narrow_sem.at[c])
        store.start()
        stores.append(store)
    onehot = (lax.broadcasted_iota(jnp.int32, (32, SLOTS), 0) == col_ids[...]).astype(BF16)
    count[...] = jnp.dot(onehot, sums[...].astype(BF16), preferred_element_type=F32)
    near = send(count, sib_count, c_send.at[n], c_recv.at[n], sibling, col)
    near.start()
    forwards = []
    for k in range(n):
        own[k].wait_recv()
        block = feats.at[frm[k]]
        forward = send(block, block, g_send.at[k], g_recv.at[k], sibling, col)
        forward.start()
        forwards.append(forward)
    near.wait()
    pair[...] = count[...] + sib_count[...]
    far = [send(pair, far_count.at[k], c_send.at[k], c_recv.at[k], to[k], col) for k in range(n)]
    for copy in far:
        copy.start()
    total = pair[...]
    for k in range(n):
        far[k].wait_recv()
        total = total + far_count[k]
    scale = 1.0 / jnp.sqrt(1.0 + total)
    scale_out[...] = scale
    turned = jnp.transpose(jnp.concatenate([scale, jnp.zeros((96, T), F32)], axis=0))
    own[n].wait_recv()
    for k in range(n):
        forwards[k].wait_recv()
    for t in range(32):
        block = feats[t // 2, pl.ds((t % 2) * T, T), :].astype(F32)
        scaled_out[t] = (block * turned[:, t:t + 1]).astype(BF16)
    for copy in own + forwards + far:
        copy.wait_send()
    for store in stores:
        store.wait()


def forward_kernel(row_ids, col_ids, narrow, scaled, out, count_out, acc, hits):
    step = pl.program_id(0)

    @pl.when(step == 0)
    def _():
        acc[...] = jnp.zeros_like(acc)
        hits[...] = jnp.zeros_like(hits)

    for g in range(CHUNK // 4):
        terms = []
        for i in range(4):
            s = g * 4 + i
            terms.append(
                jnp.dot(narrow[s], scaled[col_ids[step * CHUNK + s]], preferred_element_type=F32)
            )
        for i in range(4):
            s = g * 4 + i
            r = row_ids[step * CHUNK + s]
            acc[r] += terms[i]
            hits[r] += narrow[s]

    @pl.when(step == pl.num_programs(0) - 1)
    def _():
        out[...] = acc[...].astype(BF16)
        ones = jnp.ones((8, T), BF16)
        for t in range(32):
            row_sum = lax.dot_general(
                ones, hits[t], (((1,), (1,)), ((), ())), preferred_element_type=F32
            )
            count_out[pl.ds(t, 1), :] = row_sum[0:1]


def middle_kernel(
    part, row_part, weight, bias, cot,
    act_out, back_out, grad_out,
    x_in, x_sum, z_in, cx_in, c_sum, cz_in, grads, gx_in, gz_buf, gz_in, back,
    xs, xr, zs, zr, cxs, cxr, czs, czr, gxs, gxr, gzs, gzr, hzs, hzr, hxs, hxr, local_sem,
):
    row, col = lax.axis_index("row"), lax.axis_index("col")
    x, z = col // 4, col % 4

    def x_to(d):
        return (x + d) % 4

    def z_to(d):
        return (z + d) % 4

    peers_x = [x_to(d) * 4 + z for d in (1, 2, 3)]
    peers_z = [x * 4 + z_to(d) for d in (1, 2, 3)]
    greet([(row, p) for p in peers_x + peers_z])
    cx = []
    for k in range(3):
        cx.append(send(row_part.at[x_to(k + 1)], cx_in.at[k], cxs.at[k], cxr.at[k], row, peers_x[k]))
        cx[k].start()
    order = (2, 1, 3, 0)
    sends_x = {}
    for e in order:
        zc = z_to(e)
        for k in (1, 0, 2):
            copy = send(
                part.at[x_to(k + 1) * 4 + zc], x_in.at[k, e], xs.at[k, e], xr.at[k, e],
                row, peers_x[k],
            )
            copy.start()
            sends_x[k, e] = copy
    total_count = row_part[x]
    for k in range(3):
        cx[k].wait_recv()
        total_count = total_count + cx_in[k]
    c_sum[...] = total_count
    cz = []
    for k in range(3):
        cz.append(send(c_sum, cz_in.at[k], czs.at[k], czr.at[k], row, peers_z[k]))
        cz[k].start()
    sends_z = []
    agg = None
    for e in order:
        for k in range(3):
            sends_x[k, e].wait_recv()
        total = part[x * 4 + z_to(e)].astype(F32)
        for k in range(3):
            total = total + x_in[k, e].astype(F32)
        if e == 0:
            agg = total
        else:
            x_sum[e - 1] = total.astype(BF16)
            copy = send(x_sum.at[e - 1], z_in.at[e - 1], zs.at[e - 1], zr.at[e - 1], row, peers_z[e - 1])
            copy.start()
            sends_z.append(copy)
    total_count = c_sum[...]
    for k in range(3):
        cz[k].wait_recv()
        total_count = total_count + cz_in[k]
    cx_in[0] = 1.0 / jnp.sqrt(1.0 + total_count)
    turned = [
        jnp.transpose(jnp.broadcast_to(cx_in[0, pl.ds(2 * z + h, 1), :], (T, T))) for h in range(2)
    ]
    scale = jnp.concatenate(turned, axis=0)
    scale = jnp.concatenate([scale, scale], axis=1)
    for copy in sends_z:
        copy.wait_recv()
    for k in range(3):
        agg = agg + z_in[k].astype(F32)
    summed = split_dot(agg, weight[...])
    pre = scale * summed + bias[...]
    sig = jax.nn.sigmoid(pre)
    act_out[...] = (pre * sig).astype(BF16)
    grad_pre = cot[...].astype(F32) * sig * (1.0 + pre * (1.0 - sig))
    sent = (scale * grad_pre).astype(BF16)
    turned_back = lax.dot_general(
        weight[...], sent, (((1,), (1,)), ((), ())), preferred_element_type=F32
    ).astype(BF16)
    back[0] = turned_back[:, :T]
    back[1] = turned_back[:, T:]
    mine = back_out.at[col]
    keep = pltpu.make_async_copy(back, mine, local_sem)
    keep.start()
    hz, hx = [], []
    for k in range(3):
        hz.append(send(back, mine, hzs.at[k], hzr.at[k], row, peers_z[k]))
        hz[k].start()
    for k in (1, 0, 2):
        copy = send(back, mine, hxs.at[k, 0], hxr.at[k, 0], row, peers_x[k])
        copy.start()
        hx.append(copy)
    weight_term = split_dot(jnp.transpose(agg), sent)
    bias_term = jnp.broadcast_to(jnp.sum(grad_pre, axis=0, keepdims=True), (8, 256))
    for c in range(4):
        for e in range(4):
            at = (c * 4 + e) * 8
            grads[c, e] = weight_term[at:at + 8]
        grads[c, 4] = bias_term
    gx = []
    for k in range(3):
        gx.append(send(grads.at[x_to(k + 1)], gx_in.at[k], gxs.at[k], gxr.at[k], row, peers_x[k]))
        gx[k].start()
    for k in range(3):
        hz[k].wait_recv()
        src = back_out.at[x * 4 + (z - k - 1 + 4) % 4]
        for j in (1, 0, 2):
            copy = send(src, src, hxs.at[j, k + 1], hxr.at[j, k + 1], row, peers_x[j])
            copy.start()
            hx.append(copy)
    total = grads[x]
    for k in range(3):
        gx[k].wait_recv()
        total = total + gx_in[k]
    for e in range(4):
        gz_buf[e, 0] = total[e]
        gz_buf[e, 1] = total[4]
    gz = []
    for k in range(3):
        gz.append(send(gz_buf.at[z_to(k + 1)], gz_in.at[k], gzs.at[k], gzr.at[k], row, peers_z[k]))
        gz[k].start()
    total = gz_buf[z]
    for k in range(3):
        gz[k].wait_recv()
        total = total + gz_in[k]
    grad_out[...] = total
    for copy in hx:
        copy.wait_recv()
    keep.wait()
    for copy in cx + cz + list(sends_x.values()) + sends_z + hz + hx + gx + gz:
        copy.wait_send()


def backward_kernel(row_ids, col_ids, narrow, back, out, acc):
    step = pl.program_id(0)

    @pl.when(step == 0)
    def _():
        acc[...] = jnp.zeros_like(acc)

    for g in range(CHUNK // 4):
        terms = []
        for i in range(4):
            s = g * 4 + i
            terms.append(
                jnp.dot(back[row_ids[step * CHUNK + s]], narrow[s], preferred_element_type=F32)
            )
        for i in range(4):
            s = g * 4 + i
            acc[col_ids[step * CHUNK + s]] += terms[i]

    @pl.when(step == pl.num_programs(0) - 1)
    def _():
        out[...] = acc[...].astype(BF16)


def finish_kernel(
    factor, part, scale, grad,
    feat_out, weight_out, bias_out,
    sib_in, pair, far_in, gsib_in, gpair, gfar_in, gall,
    ss, sr, fs, fr, gss, gsr, gfs, gfr, gzs, gzr, gxs, gxr,
):
    row, col = lax.axis_index("row"), lax.axis_index("col")
    zl, y, core = row_place()
    x, z = col // 4, col % 4
    sibling = row_at(zl, y, 1 - core)
    to = [row_at((zl + dz) % 2, (y + dy) % 4, core) for dz, dy in ROW_STEPS]
    n = len(ROW_STEPS)
    peers_x = [((x + d) % 4) * 4 + z for d in (1, 2, 3)]
    peers_z = [x * 4 + (z + d) % 4 for d in (1, 2, 3)]
    greet(
        [(sibling, col)] + [(p, col) for p in to] + [(row, p) for p in peers_x + peers_z]
    )
    gnear = send(grad, gsib_in, gss, gsr, sibling, col)
    gnear.start()
    near = []
    for q in range(8):
        copy = send(part.at[q, 1 - core], sib_in.at[q], ss.at[q], sr.at[q], sibling, col)
        copy.start()
        near.append(copy)
    gnear.wait()
    gpair[...] = grad[...] + gsib_in[...]
    gfar = []
    for k in range(n):
        gfar.append(send(gpair, gfar_in.at[k], gfs.at[k], gfr.at[k], to[k], col))
        gfar[k].start()
    for copy in near:
        copy.wait()

    def pair_sum(q, carry):
        pair[q] = (part[q, core].astype(F32) + sib_in[q].astype(F32)).astype(BF16)
        return carry

    lax.fori_loop(0, 8, pair_sum, 0)
    far = []
    for k, (dz, dy) in enumerate(ROW_STEPS):
        q = ((zl + dz) % 2) * 4 + (y + dy) % 4
        far.append(send(pair.at[q], far_in.at[k], fs.at[k], fr.at[k], to[k], col))
        far[k].start()
    total = gpair[...]
    for k in range(n):
        gfar[k].wait_recv()
        total = total + gfar_in[k]
    total = total * factor
    gall[col] = total[0]
    bias_out[...] = total[1, 0:1]
    mine = gall.at[col]
    gz, gx = [], []
    for k in range(3):
        gz.append(send(mine, mine, gzs.at[k], gzr.at[k], row, peers_z[k]))
        gz[k].start()
    for k in range(3):
        gx.append(send(mine, mine, gxs.at[k, 0], gxr.at[k, 0], row, peers_x[k]))
        gx[k].start()
    for k in range(3):
        gz[k].wait_recv()
        src = gall.at[x * 4 + (z - k - 1 + 4) % 4]
        for j in range(3):
            copy = send(src, src, gxs.at[j, k + 1], gxr.at[j, k + 1], row, peers_x[j])
            copy.start()
            gx.append(copy)
    block = pair[zl * 4 + y].astype(F32)
    for k in range(n):
        far[k].wait_recv()
        block = block + far_in[k].astype(F32)
    for h in range(2):
        scaled = block[h] * scale[pl.ds(row * 2 + h, 1), :]
        feat_out[pl.ds(h * T, T), :] = jnp.transpose(scaled).astype(BF16)
    for copy in gx:
        copy.wait_recv()
    for c in range(16):
        weight_out[pl.ds(c * 8, 8), :] = gall[c]
    for copy in gfar + far + gz + gx:
        copy.wait_send()


def params(collective_id=None):
    if collective_id is None:
        return pltpu.CompilerParams(
            vmem_limit_bytes=VMEM_LIMIT, dimension_semantics=("arbitrary",)
        )
    return pltpu.CompilerParams(
        vmem_limit_bytes=VMEM_LIMIT, has_side_effects=True, collective_id=collective_id
    )


def on_device(features, weight, bias, cotangent, tile_rows, tile_cols, tile_mask):
    nodes = features.shape[0] * lax.axis_size("row") * lax.axis_size("col")
    row_ids = tile_rows.reshape(SLOTS)
    col_ids = tile_cols.reshape(SLOTS)
    mask = tile_mask.reshape(SLOTS, T, T)
    vmem = pl.BlockSpec(memory_space=pltpu.VMEM)
    hbm = pl.BlockSpec(memory_space=pl.ANY)
    dma = pltpu.SemaphoreType.DMA
    shape = jax.ShapeDtypeStruct
    n = len(ROW_STEPS)
    chunks = SLOTS // CHUNK

    narrow, scaled, scale = pl.pallas_call(
        spread_kernel,
        out_shape=(
            shape((SLOTS, T, T), BF16),
            shape((32, T, T), BF16),
            shape((32, T), F32),
        ),
        in_specs=[vmem, vmem, hbm],
        out_specs=(hbm, vmem, vmem),
        scratch_shapes=[
            pltpu.VMEM((SLOTS, T, T), jnp.int32),
            pltpu.VMEM((SLOTS, T, T), BF16),
            pltpu.VMEM((16, 256, T), BF16),
            pltpu.VMEM((SLOTS, T), F32),
            pltpu.VMEM((32, T), F32),
            pltpu.VMEM((32, T), F32),
            pltpu.VMEM((32, T), F32),
            pltpu.VMEM((n, 32, T), F32),
            dma((chunks,)), dma((chunks,)),
            dma((n + 1,)), dma((n + 1,)), dma((n,)), dma((n,)), dma((n + 1,)), dma((n + 1,)),
        ],
        compiler_params=params(1),
        name="spread",
    )(features, col_ids.reshape(1, SLOTS), mask)

    tile_block = pl.BlockSpec((CHUNK, T, T), lambda i, *_: (i, 0, 0))
    whole = pl.BlockSpec((32, T, T), lambda i, *_: (0, 0, 0))
    part, row_part = pl.pallas_call(
        forward_kernel,
        out_shape=(shape((32, T, T), BF16), shape((32, T), F32)),
        grid_spec=pltpu.PrefetchScalarGridSpec(
            num_scalar_prefetch=2,
            grid=(chunks,),
            in_specs=[tile_block, whole],
            out_specs=[whole, pl.BlockSpec((32, T), lambda i, *_: (0, 0))],
            scratch_shapes=[pltpu.VMEM((32, T, T), F32), pltpu.VMEM((32, T, T), BF16)],
        ),
        compiler_params=params(),
        name="forward",
    )(row_ids, col_ids, narrow, scaled)

    activations, back, grad_part = pl.pallas_call(
        middle_kernel,
        out_shape=(
            shape((256, 256), BF16),
            shape((16, 2, T, T), BF16),
            shape((2, 8, 256), F32),
        ),
        in_specs=[vmem] * 5,
        out_specs=(vmem, hbm, vmem),
        scratch_shapes=[
            pltpu.VMEM((3, 4, 256, T), BF16),
            pltpu.VMEM((3, 256, T), BF16),
            pltpu.VMEM((3, 256, T), BF16),
            pltpu.VMEM((3, 8, T), F32),
            pltpu.VMEM((8, T), F32),
            pltpu.VMEM((3, 8, T), F32),
            pltpu.VMEM((4, 5, 8, 256), F32),
            pltpu.VMEM((3, 5, 8, 256), F32),
            pltpu.VMEM((4, 2, 8, 256), F32),
            pltpu.VMEM((3, 2, 8, 256), F32),
            pltpu.VMEM((2, T, T), BF16),
            dma((3, 4)), dma((3, 4)), dma((3,)), dma((3,)),
            dma((3,)), dma((3,)), dma((3,)), dma((3,)),
            dma((3,)), dma((3,)), dma((3,)), dma((3,)),
            dma((3,)), dma((3,)), dma((3, 4)), dma((3, 4)),
            dma,
        ],
        compiler_params=params(2),
        name="middle",
    )(part.reshape(16, 256, T), row_part.reshape(4, 8, T), weight, bias.reshape(1, 256), cotangent)

    column_part = pl.pallas_call(
        backward_kernel,
        out_shape=shape((32, T, T), BF16),
        grid_spec=pltpu.PrefetchScalarGridSpec(
            num_scalar_prefetch=2,
            grid=(chunks,),
            in_specs=[tile_block, whole],
            out_specs=whole,
            scratch_shapes=[pltpu.VMEM((32, T, T), F32)],
        ),
        compiler_params=params(),
        name="backward",
    )(row_ids, col_ids, narrow, back.reshape(32, T, T))

    factor = 1.0 / float(nodes) ** 0.5
    grad_features, grad_weight, grad_bias = pl.pallas_call(
        functools.partial(finish_kernel, factor),
        out_shape=(
            shape((256, T), BF16),
            shape((T, 256), F32),
            shape((1, 256), F32),
        ),
        in_specs=[vmem] * 3,
        out_specs=(vmem, vmem, vmem),
        scratch_shapes=[
            pltpu.VMEM((8, 2, T, T), BF16),
            pltpu.VMEM((8, 2, T, T), BF16),
            pltpu.VMEM((n, 2, T, T), BF16),
            pltpu.VMEM((2, 8, 256), F32),
            pltpu.VMEM((2, 8, 256), F32),
            pltpu.VMEM((n, 2, 8, 256), F32),
            pltpu.VMEM((16, 8, 256), F32),
            dma((8,)), dma((8,)), dma((n,)), dma((n,)),
            dma, dma, dma((n,)), dma((n,)),
            dma((3,)), dma((3,)), dma((3, 4)), dma((3, 4)),
        ],
        compiler_params=params(3),
        name="finish",
    )(column_part.reshape(8, 2, 2, T, T), scale, grad_part)
    return (activations, grad_features, grad_weight, grad_bias.reshape(256))


def solution(mesh):
    placed = (
        P(("col", "row"), None),
        P(),
        P(),
        P(("row", "col"), None),
        P("row", "col", None),
        P("row", "col", None),
        P("row", "col", None, None, None),
    )
    return jax.shard_map(
        on_device,
        mesh=mesh,
        in_specs=placed,
        out_specs=(P(("row", "col"), None), P(("col", "row"), None), P(), P()),
        check_vma=False,
    )
```

```python
import functools

import jax
import jax.numpy as jnp
from jax import lax
from jax.experimental import pallas as pl
from jax.experimental.pallas import tpu as pltpu
from jax.sharding import PartitionSpec as P

F32 = jnp.float32
BF16 = jnp.bfloat16
T = 128
SLOTS = 160
CHUNK = 16
GROUP = 16
PAIRS = (SLOTS + 32) // 2
COPIES = 102
VMEM_LIMIT = 56 * 1024 * 1024
ROW_STEPS = tuple((dz, dy) for dz in (1, 0) for dy in (2, 1, 3, 0) if (dz, dy) != (0, 0))
NEAR = (1, 0, 2)


class Links:
    def __init__(self, send_sems, recv_sems):
        self.send_sems, self.recv_sems = send_sems, recv_sems
        self.started = []

    def send(self, src, dst, device):
        k = len(self.started)
        copy = pltpu.make_async_remote_copy(
            src_ref=src,
            dst_ref=dst,
            send_sem=self.send_sems.at[k],
            recv_sem=self.recv_sems.at[k],
            device_id=device,
            device_id_type=pl.DeviceIdType.MESH,
        )
        copy.start()
        self.started.append(copy)
        return copy

    def drain(self):
        for copy in self.started:
            copy.wait_send()


def split_dot(a, b):
    hi = a.astype(BF16)
    lo = (a - hi.astype(F32)).astype(BF16)
    return jnp.dot(hi, b, preferred_element_type=F32) + jnp.dot(lo, b, preferred_element_type=F32)


def sort_lists(ids, others, lists, at):
    lane = lax.broadcasted_iota(jnp.int32, (1, 256), 1)
    key = (jnp.where(lane < SLOTS, ids, 64) * 256 + lane).astype(F32)
    along = jnp.broadcast_to(key, (256, 256))
    down = jnp.transpose(along)
    wide_lane = lax.broadcasted_iota(jnp.int32, (256, 256), 1).astype(F32)
    id_down = jnp.floor(down * (1.0 / 256.0))
    rank = jnp.sum((along < down).astype(F32), axis=1, keepdims=True)
    held = jnp.sum((id_down == wide_lane).astype(F32), axis=0, keepdims=True)
    odd = held - 2.0 * jnp.floor(held * 0.5)
    below = jnp.sum(jnp.where(wide_lane < id_down, odd, 0.0), axis=1, keepdims=True)
    pos = rank + below
    first = 1.0 - (pos - 2.0 * jnp.floor(pos * 0.5))
    place = jnp.where(id_down < 63.0, (pos == wide_lane).astype(F32), 0.0).astype(BF16)
    row = lax.broadcasted_iota(jnp.int32, (8, 256), 0)
    values = jnp.where(row == 0, lane + 1, jnp.where(row == 1, others, ids))
    moved = jnp.dot(values.astype(F32).astype(BF16), place, preferred_element_type=F32)
    upto = jnp.where(id_down <= wide_lane, first, 0.0)
    last = jnp.sum(upto, axis=0, keepdims=True) - 1.0
    found = jnp.where(row == 3, last, moved).astype(jnp.int32)
    least = jnp.where(row == 3, -1, 0)
    most = jnp.where(row == 0, SLOTS, jnp.where(row == 3, PAIRS - 1, 31))
    lists[pl.ds(at, 8), :] = jnp.minimum(jnp.maximum(found, least), most)


def layer_kernel(
    factor,
    feat, weight_hbm, bias_hbm, cot_hbm, row_hbm, col_hbm, mask,
    act_out, feat_out, weight_out, bias_out,
    weight, bias, cot, row_ids, col_ids,
    mask_in, narrow, running, padded, lists_v, lists,
    feats, sums, count, sib_count, pair_count, far_count,
    row_count, rx_in, rx_sum, rz_in, scaled,
    part, x_in, z_buf, z_in, back,
    scale_keep, row_scale, grads, gsib_in, gq_buf, gq_in, gx_buf, gz_buf, gall,
    col_part, sib_in, pair, far_in,
    mask_sem, list_sem, in_sem, send_sems, recv_sems,
):
    row, col = lax.axis_index("row"), lax.axis_index("col")
    zl, y, core = row // 8, (row // 2) % 4, row % 2
    x, z = col // 4, col % 4
    here = zl * 4 + y
    sibling = (zl * 8 + y * 2 + 1 - core, col)
    row_to = [(((zl + dz) % 2) * 8 + ((y + dy) % 4) * 2 + core, col) for dz, dy in ROW_STEPS]
    row_from = [((zl - dz + 2) % 2) * 4 + (y - dy + 4) % 4 for dz, dy in ROW_STEPS]
    far = len(ROW_STEPS)
    x_at = [(x + d) % 4 for d in (1, 2, 3)]
    z_at = [(z + d) % 4 for d in (1, 2, 3)]
    x_to = [(row, p * 4 + z) for p in x_at]
    z_to = [(row, x * 4 + p) for p in z_at]
    x_from = [(x - d + 4) % 4 for d in (1, 2, 3)]
    z_from = [(z - d + 4) % 4 for d in (1, 2, 3)]
    links = Links(send_sems, recv_sems)
    send = links.send

    barrier = pltpu.get_barrier_semaphore()
    peers = [sibling] + row_to + x_to + z_to
    for device in peers:
        pl.semaphore_signal(
            barrier, inc=1, device_id=device, device_id_type=pl.DeviceIdType.MESH
        )
    chunks = SLOTS // CHUNK
    loads = []
    held_in = []
    for k, (src, dst) in enumerate(
        (
            (row_hbm, row_ids),
            (col_hbm, col_ids),
            (feat, feats.at[core, here]),
            (weight_hbm, weight),
            (bias_hbm, bias),
            (cot_hbm, cot),
        )
    ):
        held_in.append(pltpu.make_async_copy(src, dst, in_sem.at[k]))
    for copy in held_in[:2]:
        copy.start()
    for c in range(chunks):
        span = pl.ds(c * CHUNK, CHUNK)
        load = pltpu.make_async_copy(mask.at[span], mask_in.at[span], mask_sem.at[c])
        load.start()
        loads.append(load)
        if c == 1:
            for copy in held_in[2:]:
                copy.start()

    narrow[0] = jnp.zeros((T, T), BF16)

    def take(c):
        loads[c].wait()

        def eight(g, carry):
            at = pl.multiple_of(c * CHUNK + g * 8, 8)
            wide = mask_in[pl.ds(at, 8)].astype(F32)
            narrow[pl.ds(at + 1, 8)] = wide.astype(BF16)
            sums[pl.ds(at, 8), :] = jnp.sum(wide, axis=1)
            return carry

        lax.fori_loop(0, CHUNK // 8, eight, 0)

    for c in range(chunks // 2):
        take(c)
    pl.semaphore_wait(barrier, len(peers))
    held_in[2].wait()
    mine = feats.at[core, here]
    own = [send(mine, mine, device) for device in row_to + [sibling]]
    for c in range(chunks // 2, chunks):
        take(c)
    slot_row = lax.broadcasted_iota(jnp.int32, (32, SLOTS), 0)
    for copy in held_in[:2]:
        copy.wait()
    onehot = (slot_row == col_ids[...]).astype(BF16)
    count[...] = jnp.dot(onehot, sums[...].astype(BF16), preferred_element_type=F32)
    near = send(count, sib_count, sibling)

    near.wait_recv()
    pair_count[...] = count[...] + sib_count[...]
    far_counts = [send(pair_count, far_count.at[k], row_to[k]) for k in range(far)]
    padded[...] = jnp.zeros_like(padded)
    padded[0:1, 0:SLOTS] = row_ids[...]
    padded[8:9, 0:SLOTS] = col_ids[...]
    rows_wide, cols_wide = padded[0:1, :], padded[8:9, :]
    sort_lists(rows_wide, cols_wide, lists_v, 0)
    sort_lists(cols_wide, rows_wide, lists_v, 8)
    list_copy = pltpu.make_async_copy(lists_v, lists, list_sem)
    list_copy.start()
    ones = jnp.ones((8, T), BF16)

    def row_sums(g, carry):
        at = pl.multiple_of(g * 8, 8)
        tiles = narrow[pl.ds(at + 1, 8)].reshape(8 * T, T)
        got = lax.dot_general(ones, tiles, (((1,), (1,)), ((), ())), preferred_element_type=F32)
        sums[pl.ds(at, 8), :] = jnp.concatenate(
            [got[0:1, i * T:(i + 1) * T] for i in range(8)], axis=0
        )
        return carry

    lax.fori_loop(0, SLOTS // 8, row_sums, 0)
    onehot = (slot_row == row_ids[...]).astype(BF16)
    got = jnp.dot(onehot, sums[...].astype(BF16), preferred_element_type=F32)
    for c in range(4):
        row_count[c] = got[c * 8:c * 8 + 8]
    rx = [send(row_count.at[x_at[k]], rx_in.at[k], x_to[k]) for k in range(3)]
    forwards = []
    for k in range(far):
        own[k].wait_recv()
        block = feats.at[core, row_from[k]]
        forwards.append(send(block, block, sibling))
    total = pair_count[...]
    for k in range(far):
        far_counts[k].wait_recv()
        total = total + far_count[k]
    col_scale = 1.0 / jnp.sqrt(1.0 + total)
    scale_keep[...] = col_scale
    turned = jnp.transpose(jnp.concatenate([col_scale, jnp.zeros((96, T), F32)], axis=0))
    own[far].wait_recv()
    for copy in forwards:
        copy.wait_recv()
    for t in range(32):
        block = feats[(t // 2) % 2, t // 4, pl.ds((t % 2) * T, T), :].astype(F32)
        scaled[t] = (block * turned[:, t:t + 1]).astype(BF16)

    list_copy.wait()

    def products(at, term, begin, end, acc):
        def group(g, acc):
            terms = [term(g * GROUP + i) for i in range(GROUP)]
            for i in range(GROUP):
                p = g * GROUP + i
                same = lists[at + 2, 2 * p] == lists[at + 2, 2 * jnp.maximum(p - 1, 0)]
                acc = jnp.where(same, acc, 0.0) + terms[i]
                running[p] = acc
            return acc

        return lax.fori_loop(begin // GROUP, end // GROUP, group, acc)

    def tile_sum(at, t):
        last = lists[at + 3, t]
        before = jnp.where(t > 0, lists[at + 3, jnp.maximum(t - 1, 0)], -1)
        return jnp.where(last > before, running[jnp.maximum(last, 0)], 0.0)

    def forward_term(p):
        spots = [(lists[0, 2 * p + i], lists[1, 2 * p + i]) for i in range(2)]
        left = jnp.concatenate([narrow[s] for s, _ in spots], axis=1)
        right = jnp.concatenate([scaled[c] for _, c in spots], axis=0)
        return jnp.dot(left, right, preferred_element_type=F32)

    products(0, forward_term, 0, PAIRS, jnp.zeros((T, T), F32))

    def put_part(t, carry):
        part[t % 2, t // 2] = tile_sum(0, t).astype(BF16)
        return carry

    lax.fori_loop(0, 32, put_part, 0)
    x_sends = []
    for h in range(2):
        got = {}
        for k in NEAR:
            got[k] = send(part.at[h, pl.ds(x_at[k] * 4, 4)], x_in.at[k, h], x_to[k])
        x_sends.append(got)

    total = row_count[x]
    for k in range(3):
        rx[k].wait_recv()
        total = total + rx_in[k]
    rx_sum[...] = total
    rz = [send(rx_sum, rz_in.at[k], z_to[k]) for k in range(3)]

    def x_total(h):
        for k in NEAR:
            x_sends[h][k].wait_recv()
        z_sends = {}
        for e in (2, 1, 3, 0):
            zc = z if e == 0 else z_at[e - 1]
            total = tile_sum(0, (x * 4 + zc) * 2 + h)
            for k in range(3):
                total = total + x_in[k, h, zc].astype(F32)
            if e:
                z_buf[h, e - 1] = total.astype(BF16)
                z_sends[e - 1] = send(z_buf.at[h, e - 1], z_in.at[h, e - 1], z_to[e - 1])
        return total, z_sends

    def activate(h, total, z_sends, scale):
        for k in range(3):
            z_sends[k].wait_recv()
            total = total + z_in[h, k].astype(F32)
        span = pl.ds(h * T, T)
        pre = scale * split_dot(total, weight[...]) + bias[...]
        sig = jax.nn.sigmoid(pre)
        act_out[span, :] = (pre * sig).astype(BF16)
        grad_pre = cot[span, :].astype(F32) * sig * (1.0 + pre * (1.0 - sig))
        sent = (scale * grad_pre).astype(BF16)
        back[h, col] = lax.dot_general(
            weight[...], sent, (((1,), (1,)), ((), ())), preferred_element_type=F32
        ).astype(BF16)
        mine = back.at[h, col]
        hz = [send(mine, mine, z_to[k]) for k in range(3)]
        hx = [send(mine, mine, x_to[k]) for k in NEAR]
        return total, sent, jnp.sum(grad_pre, axis=0, keepdims=True), hz, hx

    def pass_on(h, hz, hx):
        for k in NEAR[::-1]:
            hz[k].wait_recv()
            block = back.at[h, x * 4 + z_from[k]]
            hx.extend(send(block, block, x_to[j]) for j in NEAR)

    agg0, z_sends0 = x_total(0)
    total = rx_sum[...]
    for k in range(3):
        rz[k].wait_recv()
        total = total + rz_in[k]
    row_scale[...] = 1.0 / jnp.sqrt(1.0 + total)
    scales = []
    for h in range(2):
        turned = jnp.transpose(jnp.broadcast_to(row_scale[pl.ds(2 * z + h, 1), :], (T, T)))
        scales.append(jnp.concatenate([turned, turned], axis=1))
    for copy in held_in[3:]:
        copy.wait()
    agg0, sent0, bias0, hz0, hx0 = activate(0, agg0, z_sends0, scales[0])
    agg1, z_sends1 = x_total(1)
    pass_on(0, hz0, hx0)
    agg1, sent1, bias1, hz1, hx1 = activate(1, agg1, z_sends1, scales[1])

    weight_term = split_dot(jnp.transpose(agg0), sent0) + split_dot(jnp.transpose(agg1), sent1)
    bias_term = jnp.broadcast_to(bias0 + bias1, (8, 256))
    for c in range(2):
        for q in range(8):
            at = (q * 2 + c) * 8
            grads[c, q] = weight_term[at:at + 8]
        grads[c, 8] = bias_term
    gsib = send(grads.at[1 - core], gsib_in, sibling)
    pass_on(1, hz1, hx1)
    gsib.wait_recv()
    for q in range(8):
        gq_buf[q, 0] = grads[core, q] + gsib_in[q]
        gq_buf[q, 1] = grads[core, 8] + gsib_in[8]
    gq_in[here] = gq_buf[here]
    gq = []
    for k, (dz, dy) in enumerate(ROW_STEPS):
        there = ((zl + dz) % 2) * 4 + (y + dy) % 4
        gq.append(send(gq_buf.at[there], gq_in.at[here], row_to[k]))
    for copy in hx0 + hx1:
        copy.wait_recv()

    for copy in gq:
        copy.wait_recv()
    total = gq_in[0]
    for q in range(1, 8):
        total = total + gq_in[q]
    gx_buf[x] = total
    gx = [send(gx_buf.at[x], gx_buf.at[x], x_to[k]) for k in range(3)]

    def backward_term(p):
        spots = [(lists[8, 2 * p + i], lists[9, 2 * p + i]) for i in range(2)]
        left = jnp.concatenate([back[r % 2, r // 2] for _, r in spots], axis=1)
        right = jnp.concatenate([narrow[s] for s, _ in spots], axis=0)
        return jnp.dot(left, right, preferred_element_type=F32)

    acc = products(8, backward_term, 0, PAIRS // 2, jnp.zeros((T, T), F32))
    for copy in gx:
        copy.wait_recv()
    gz_buf[z] = (gx_buf[0] + gx_buf[1]) + (gx_buf[2] + gx_buf[3])
    gz = [send(gz_buf.at[z], gz_buf.at[z], z_to[k]) for k in range(3)]
    products(8, backward_term, PAIRS // 2, PAIRS, acc)

    near = {}
    for dz in (1, 0):
        half = (zl + dz) % 2

        def put_col(i, carry):
            q = half * 4 + i // 2
            col_part[q, i % 2] = tile_sum(8, q * 4 + (1 - core) * 2 + i % 2).astype(BF16)
            return carry

        lax.fori_loop(0, 8, put_col, 0)
        span = pl.ds(half * 4, 4)
        near[dz] = send(col_part.at[span], sib_in.at[span], sibling)
    far_sends = []

    def pair_up(k, dz, dy):
        q = ((zl + dz) % 2) * 4 + (y + dy) % 4
        for h in range(2):
            both = tile_sum(8, q * 4 + core * 2 + h) + sib_in[q, h].astype(F32)
            pair[k, h] = both.astype(BF16)
        far_sends.append(send(pair.at[k], far_in.at[k], row_to[k]))

    near[1].wait_recv()
    for k, (dz, dy) in enumerate(ROW_STEPS):
        if dz == 1:
            pair_up(k, dz, dy)
    for copy in gz:
        copy.wait_recv()
    total = ((gz_buf[0] + gz_buf[1]) + (gz_buf[2] + gz_buf[3])) * factor
    gall[core, here] = total[0]
    bias_out[...] = total[1, 0:1]
    mine = gall.at[core, here]
    ga = [send(mine, mine, device) for device in row_to]
    near[0].wait_recv()
    for k, (dz, dy) in enumerate(ROW_STEPS):
        if dz == 0:
            pair_up(k, dz, dy)
    blocks = [
        tile_sum(8, here * 4 + core * 2 + h) + sib_in[here, h].astype(F32) for h in range(2)
    ]
    for copy in ga:
        copy.wait_recv()
    gs = send(gall.at[core], gall.at[core], sibling)
    for k in range(far):
        far_sends[k].wait_recv()
        blocks = [blocks[h] + far_in[k, h].astype(F32) for h in range(2)]
    for h in range(2):
        block = blocks[h] * scale_keep[pl.ds(row * 2 + h, 1), :]
        feat_out[pl.ds(h * T, T), :] = jnp.transpose(block).astype(BF16)
    gs.wait_recv()
    for c in range(2):
        for q in range(8):
            weight_out[pl.ds((q * 2 + c) * 8, 8), :] = gall[c, q]
    links.drain()
    assert len(links.started) == COPIES


def emit_kernel(*refs):
    for src, dst in zip(refs[:4], refs[4:]):
        dst[...] = src[...]


def on_device(features, weight, bias, cotangent, tile_rows, tile_cols, tile_mask):
    nodes = features.shape[0] * lax.axis_size("row") * lax.axis_size("col")
    vmem = pl.BlockSpec(memory_space=pltpu.VMEM)
    dma = pltpu.SemaphoreType.DMA
    shape = jax.ShapeDtypeStruct
    far = len(ROW_STEPS)
    outs = (
        shape((256, 256), BF16),
        shape((256, T), BF16),
        shape((T, 256), F32),
        shape((1, 256), F32),
    )
    results = pl.pallas_call(
        functools.partial(layer_kernel, 1.0 / float(nodes) ** 0.5),
        out_shape=outs,
        in_specs=[pl.BlockSpec(memory_space=pltpu.HBM)] * 7,
        out_specs=(vmem,) * 4,
        scratch_shapes=[
            pltpu.VMEM((T, 256), BF16),
            pltpu.VMEM((1, 256), F32),
            pltpu.VMEM((256, 256), BF16),
            pltpu.VMEM((1, SLOTS), jnp.int32),
            pltpu.VMEM((1, SLOTS), jnp.int32),
            pltpu.VMEM((SLOTS, T, T), jnp.int32),
            pltpu.VMEM((SLOTS + 1, T, T), BF16),
            pltpu.VMEM((PAIRS, T, T), F32),
            pltpu.VMEM((16, 256), jnp.int32),
            pltpu.VMEM((16, 256), jnp.int32),
            pltpu.SMEM((16, 256), jnp.int32),
            pltpu.VMEM((2, 8, 256, T), BF16),
            pltpu.VMEM((SLOTS, T), F32),
            pltpu.VMEM((32, T), F32),
            pltpu.VMEM((32, T), F32),
            pltpu.VMEM((32, T), F32),
            pltpu.VMEM((far, 32, T), F32),
            pltpu.VMEM((4, 8, T), F32),
            pltpu.VMEM((3, 8, T), F32),
            pltpu.VMEM((8, T), F32),
            pltpu.VMEM((3, 8, T), F32),
            pltpu.VMEM((32, T, T), BF16),
            pltpu.VMEM((2, 16, T, T), BF16),
            pltpu.VMEM((3, 2, 4, T, T), BF16),
            pltpu.VMEM((2, 3, T, T), BF16),
            pltpu.VMEM((2, 3, T, T), BF16),
            pltpu.VMEM((2, 16, T, T), BF16),
            pltpu.VMEM((32, T), F32),
            pltpu.VMEM((8, T), F32),
            pltpu.VMEM((2, 9, 8, 256), F32),
            pltpu.VMEM((9, 8, 256), F32),
            pltpu.VMEM((8, 2, 8, 256), F32),
            pltpu.VMEM((8, 2, 8, 256), F32),
            pltpu.VMEM((4, 2, 8, 256), F32),
            pltpu.VMEM((4, 2, 8, 256), F32),
            pltpu.VMEM((2, 8, 8, 256), F32),
            pltpu.VMEM((8, 2, T, T), BF16),
            pltpu.VMEM((8, 2, T, T), BF16),
            pltpu.VMEM((far, 2, T, T), BF16),
            pltpu.VMEM((far, 2, T, T), BF16),
            dma((SLOTS // CHUNK,)),
            dma,
            dma((6,)),
            dma((COPIES,)),
            dma((COPIES,)),
        ],
        compiler_params=pltpu.CompilerParams(
            vmem_limit_bytes=VMEM_LIMIT, has_side_effects=True, collective_id=1
        ),
        name="layer",
    )(
        features,
        weight,
        bias.reshape(1, 256),
        cotangent,
        tile_rows.reshape(1, SLOTS),
        tile_cols.reshape(1, SLOTS),
        tile_mask.reshape(SLOTS, T, T),
    )
    activations, grad_features, grad_weight, grad_bias = pl.pallas_call(
        emit_kernel,
        out_shape=outs,
        in_specs=[vmem] * 4,
        out_specs=(vmem,) * 4,
        name="emit",
    )(*results)
    return (activations, grad_features, grad_weight, grad_bias.reshape(256))


def solution(mesh):
    placed = (
        P(("col", "row"), None),
        P(),
        P(),
        P(("row", "col"), None),
        P("row", "col", None),
        P("row", "col", None),
        P("row", "col", None, None, None),
    )
    return jax.shard_map(
        on_device,
        mesh=mesh,
        in_specs=placed,
        out_specs=(P(("row", "col"), None), P(("col", "row"), None), P(), P()),
        check_vma=False,
    )
```

```python
import functools

import jax
import jax.numpy as jnp
from jax import lax
from jax.experimental import pallas as pl
from jax.experimental.pallas import tpu as pltpu
from jax.sharding import PartitionSpec as P

F32 = jnp.float32
BF16 = jnp.bfloat16
T = 128
SLOTS = 160
CHUNK = 16
GROUP = 16
PAIRS = (SLOTS + 32) // 2
SENDS = 48
GROUPS = 54
VMEM_LIMIT = 56 * 1024 * 1024
ROW_STEPS = tuple((dz, dy) for dz in (1, 0) for dy in (2, 1, 3, 0) if (dz, dy) != (0, 0))
NEAR = (1, 0, 2)
PIECES = 4
PIECE = 256 // PIECES


class Links:
    def __init__(self, send_sems, recv_sems):
        self.send_sems, self.recv_sems = send_sems, recv_sems
        self.open, self.starts, self.groups = {}, 0, 0

    def group(self):
        self.groups += 1
        return self.groups - 1

    def send(self, src, dst, device, group):
        k = self.starts % SENDS
        self.starts += 1
        if k in self.open:
            self.open[k].wait_send()
        copy = pltpu.make_async_remote_copy(
            src_ref=src,
            dst_ref=dst,
            send_sem=self.send_sems.at[k],
            recv_sem=self.recv_sems.at[group],
            device_id=device,
            device_id_type=pl.DeviceIdType.MESH,
        )
        copy.start()
        self.open[k] = copy

    def wait(self, group, ruler):
        pltpu.make_async_copy(ruler, ruler, self.recv_sems.at[group]).wait()

    def drain(self):
        for copy in self.open.values():
            copy.wait_send()


def split_dot(a, b):
    hi = a.astype(BF16)
    lo = (a - hi.astype(F32)).astype(BF16)
    return jnp.dot(hi, b, preferred_element_type=F32) + jnp.dot(lo, b, preferred_element_type=F32)


def sort_lists(ids, others, lists, at):
    lane = lax.broadcasted_iota(jnp.int32, (1, 256), 1)
    key = (jnp.where(lane < SLOTS, ids, 64) * 256 + lane).astype(F32)
    along = jnp.broadcast_to(key, (256, 256))
    down = jnp.transpose(along)
    wide_lane = lax.broadcasted_iota(jnp.int32, (256, 256), 1).astype(F32)
    id_down = jnp.floor(down * (1.0 / 256.0))
    rank = jnp.sum((along < down).astype(F32), axis=1, keepdims=True)
    held = jnp.sum((id_down == wide_lane).astype(F32), axis=0, keepdims=True)
    odd = held - 2.0 * jnp.floor(held * 0.5)
    below = jnp.sum(jnp.where(wide_lane < id_down, odd, 0.0), axis=1, keepdims=True)
    pos = rank + below
    first = 1.0 - (pos - 2.0 * jnp.floor(pos * 0.5))
    place = jnp.where(id_down < 63.0, (pos == wide_lane).astype(F32), 0.0).astype(BF16)
    row = lax.broadcasted_iota(jnp.int32, (8, 256), 0)
    values = jnp.where(row == 0, lane + 1, jnp.where(row == 1, others, ids))
    moved = jnp.dot(values.astype(F32).astype(BF16), place, preferred_element_type=F32)
    upto = jnp.where(id_down <= wide_lane, first, 0.0)
    last = jnp.sum(upto, axis=0, keepdims=True) - 1.0
    found = jnp.where(row == 3, last, moved).astype(jnp.int32)
    least = jnp.where(row == 3, -1, 0)
    most = jnp.where(row == 0, SLOTS, jnp.where(row == 3, PAIRS - 1, 31))
    lists[pl.ds(at, 8), :] = jnp.minimum(jnp.maximum(found, least), most)


def layer_kernel(
    factor,
    feat, weight_hbm, bias_hbm, cot_hbm, row_hbm, col_hbm, mask,
    act_out, feat_out, weight_out, bias_out,
    weight, bias, cot, row_ids, col_ids,
    mask_in, narrow, running, padded, lists_v, lists,
    feats, sums, count, sib_count, pair_count, pair_send, far_count,
    row_count, rx_in, rx_sum, rz_in, scaled,
    part, x_in, z_buf, z_in, back_in, back,
    scale_keep, row_scale, grads, gsib_in, gq_buf, gq_in, gx_buf, gz_buf, gall,
    col_part, sib_in, pair, far_in,
    mask_sem, list_sem, in_sem, send_sems, recv_sems,
):
    row, col = lax.axis_index("row"), lax.axis_index("col")
    zl, y, core = row // 8, (row // 2) % 4, row % 2
    x, z = col // 4, col % 4
    here = zl * 4 + y
    sibling = (zl * 8 + y * 2 + 1 - core, col)
    row_to = [(((zl + dz) % 2) * 8 + ((y + dy) % 4) * 2 + core, col) for dz, dy in ROW_STEPS]
    row_from = [((zl - dz + 2) % 2) * 4 + (y - dy + 4) % 4 for dz, dy in ROW_STEPS]
    far = len(ROW_STEPS)
    x_at = [(x + d) % 4 for d in (1, 2, 3)]
    z_at = [(z + d) % 4 for d in (1, 2, 3)]
    x_to = [(row, p * 4 + z) for p in x_at]
    z_to = [(row, x * 4 + p) for p in z_at]
    x_from = [(x - d + 4) % 4 for d in (1, 2, 3)]
    z_from = [(z - d + 4) % 4 for d in (1, 2, 3)]
    links = Links(send_sems, recv_sems)
    send, wait, group = links.send, links.wait, links.group

    barrier = pltpu.get_barrier_semaphore()
    peers = [sibling] + row_to + x_to + z_to
    for device in peers:
        pl.semaphore_signal(
            barrier, inc=1, device_id=device, device_id_type=pl.DeviceIdType.MESH
        )
    chunks = SLOTS // CHUNK
    loads = []
    held_in = []
    for k, (src, dst) in enumerate(
        (
            (row_hbm, row_ids),
            (col_hbm, col_ids),
            (feat, feats.at[core, here]),
            (weight_hbm, weight),
            (bias_hbm, bias),
            (cot_hbm, cot),
        )
    ):
        held_in.append(pltpu.make_async_copy(src, dst, in_sem.at[k]))
    for copy in held_in[:2]:
        copy.start()
    for c in range(chunks):
        span = pl.ds(c * CHUNK, CHUNK)
        load = pltpu.make_async_copy(mask.at[span], mask_in.at[span], mask_sem.at[c])
        load.start()
        loads.append(load)
        if c == 1:
            for copy in held_in[2:]:
                copy.start()

    narrow[0] = jnp.zeros((T, T), BF16)

    def take(c):
        loads[c].wait()

        def eight(g, carry):
            at = pl.multiple_of(c * CHUNK + g * 8, 8)
            wide = mask_in[pl.ds(at, 8)].astype(F32)
            narrow[pl.ds(at + 1, 8)] = wide.astype(BF16)
            sums[pl.ds(at, 8), :] = jnp.sum(wide, axis=1)
            return carry

        lax.fori_loop(0, CHUNK // 8, eight, 0)

    for c in range(chunks // 2):
        take(c)
    pl.semaphore_wait(barrier, len(peers))
    held_in[2].wait()
    mine = feats.at[core, here]
    own = [group() for _ in range(far + 1)]
    for k, device in enumerate(row_to + [sibling]):
        send(mine, mine, device, own[k])
    for c in range(chunks // 2, chunks):
        take(c)
    slot_row = lax.broadcasted_iota(jnp.int32, (32, SLOTS), 0)
    for copy in held_in[:2]:
        copy.wait()
    onehot = (slot_row == col_ids[...]).astype(BF16)
    count[...] = jnp.dot(onehot, sums[...].astype(BF16), preferred_element_type=F32)
    near_count = group()
    send(count, sib_count, sibling, near_count)

    wait(near_count, sib_count)
    pair_count[...] = count[...] + sib_count[...]
    pair_send[...] = (pair_count[...].astype(jnp.int32) - SLOTS * T).astype(jnp.int16)
    far_counts = group()
    for k in range(far):
        send(pair_send, far_count.at[k], row_to[k], far_counts)
    padded[...] = jnp.zeros_like(padded)
    padded[0:1, 0:SLOTS] = row_ids[...]
    padded[8:9, 0:SLOTS] = col_ids[...]
    rows_wide, cols_wide = padded[0:1, :], padded[8:9, :]
    sort_lists(rows_wide, cols_wide, lists_v, 0)
    sort_lists(cols_wide, rows_wide, lists_v, 8)
    list_copy = pltpu.make_async_copy(lists_v, lists, list_sem)
    list_copy.start()
    ones = jnp.ones((8, T), BF16)

    def row_sums(g, carry):
        at = pl.multiple_of(g * 8, 8)
        tiles = narrow[pl.ds(at + 1, 8)].reshape(8 * T, T)
        got = lax.dot_general(ones, tiles, (((1,), (1,)), ((), ())), preferred_element_type=F32)
        sums[pl.ds(at, 8), :] = jnp.concatenate(
            [got[0:1, i * T:(i + 1) * T] for i in range(8)], axis=0
        )
        return carry

    lax.fori_loop(0, SLOTS // 8, row_sums, 0)
    onehot = (slot_row == row_ids[...]).astype(BF16)
    got = jnp.dot(onehot, sums[...].astype(BF16), preferred_element_type=F32)
    for c in range(4):
        row_count[c] = got[c * 8:c * 8 + 8]
    rx = group()
    for k in range(3):
        send(row_count.at[x_at[k]], rx_in.at[k], x_to[k], rx)
    forwards = group()
    for k in range(far):
        wait(own[k], feats.at[0, 0])
        block = feats.at[core, row_from[k]]
        send(block, block, sibling, forwards)
    total = pair_count[...]
    wait(far_counts, far_count)
    for k in range(far):
        total = total + (far_count[k].astype(jnp.int32) + SLOTS * T).astype(F32)
    scale_keep[...] = 1.0 / jnp.sqrt(1.0 + total)
    parts = [
        scale_keep[pl.ds((q * 2 + c) * 2, 2), :] for c in (core, 1 - core) for q in range(8)
    ]
    turned = jnp.transpose(jnp.concatenate(parts + [jnp.zeros((96, T), F32)], axis=0))

    def scale_tiles(c, at):
        for q in range(8):
            for h in range(2):
                block = feats[c, q, pl.ds(h * T, T), :].astype(F32)
                lane = at + q * 2 + h
                scaled[(q * 2 + c) * 2 + h] = (block * turned[:, lane:lane + 1]).astype(BF16)

    scale_tiles(core, 0)
    wait(own[far], feats.at[0, 0])
    wait(forwards, feats.at[0, pl.ds(0, far)])
    scale_tiles(1 - core, 16)
    list_copy.wait()

    def half(i):
        return pl.ds(i * 64, 64)

    def products(at, term, rows, begin, end, acc):
        def group_of(g, acc):
            terms = [term(g * GROUP + i, rows) for i in range(GROUP)]
            for i in range(GROUP):
                p = g * GROUP + i
                same = lists[at + 2, 2 * p] == lists[at + 2, 2 * jnp.maximum(p - 1, 0)]
                acc = jnp.where(same, acc, 0.0) + terms[i]
                running[p, rows, :] = acc
            return acc

        return lax.fori_loop(begin // GROUP, end // GROUP, group_of, acc)

    def tile_sum(at, t, rows=pl.ds(0, T)):
        last = lists[at + 3, t]
        before = jnp.where(t > 0, lists[at + 3, jnp.maximum(t - 1, 0)], -1)
        return jnp.where(last > before, running[jnp.maximum(last, 0), rows, :], 0.0)

    def piece_sum(p, chunk):
        return tile_sum(0, chunk * 2 + p // 2, pl.ds(p % 2 * PIECE, PIECE))

    def forward_term(p, rows):
        spots = [(lists[0, 2 * p + i], lists[1, 2 * p + i]) for i in range(2)]
        left = jnp.concatenate([narrow[s, rows, :] for s, _ in spots], axis=1)
        right = jnp.concatenate([scaled[c] for _, c in spots], axis=0)
        return jnp.dot(left, right, preferred_element_type=F32)

    x_sends = [group() for _ in range(PIECES)]
    nothing = jnp.zeros((64, T), F32)
    for i in range(2):

        products(0, forward_term, half(i), 0, PAIRS, nothing)

        for p in (i, i + 2):
            for k in NEAR:
                for zc in range(4):
                    part[p, k, zc] = piece_sum(p, x_at[k] * 4 + zc).astype(BF16)
                send(part.at[p, k], x_in.at[k, p], x_to[k], x_sends[p])

    total = row_count[x]
    wait(rx, rx_in)
    for k in range(3):
        total = total + rx_in[k]
    rx_sum[...] = total
    rz = group()
    for k in range(3):
        send(rx_sum, rz_in.at[k], z_to[k], rz)

    def x_total(p):
        wait(x_sends[p], back.at[0, pl.ds(0, 6)])
        z_sends = group()
        for e in (2, 1, 3, 0):
            zc = z if e == 0 else z_at[e - 1]
            total = piece_sum(p, x * 4 + zc)
            for k in range(3):
                total = total + x_in[k, p, zc].astype(F32)
            if e:
                z_buf[p, e - 1] = total.astype(BF16)
                send(z_buf.at[p, e - 1], z_in.at[p, e - 1], z_to[e - 1], z_sends)
        return total, z_sends

    def activate(p, total, z_sends):
        wait(z_sends, z_in.at[p])
        for k in range(3):
            total = total + z_in[p, k].astype(F32)
        span = pl.ds(p * PIECE, PIECE)
        scale = scales[p // 2][p % 2 * PIECE:p % 2 * PIECE + PIECE]
        pre = scale * split_dot(total, weight[...]) + bias[...]
        sig = jax.nn.sigmoid(pre)
        act_out[span, :] = (pre * sig).astype(BF16)
        grad_pre = cot[span, :].astype(F32) * sig * (1.0 + pre * (1.0 - sig))
        sent = (scale * grad_pre).astype(BF16)
        turned = lax.dot_general(
            weight[...], sent, (((1,), (1,)), ((), ())), preferred_element_type=F32
        )
        back_in[p, col] = jnp.concatenate([turned[:64], turned[64:]], axis=1).astype(BF16)
        mine = back_in.at[p, col]
        for k in (1, 0, 2):
            send(mine, mine, z_to[k], hz[p][k])
        for k in NEAR:
            send(mine, mine, x_to[k], hx[p // 2][3])
        return total, sent, jnp.sum(grad_pre, axis=0, keepdims=True)

    hz = [[group() for _ in range(3)] for _ in range(PIECES)]
    hx = [[group() for _ in range(4)] for _ in range(2)]

    def pass_on(p):
        for k in (0, 2, 1):
            wait(hz[p][k], z_in.at[0, 0])
            block = back_in.at[p, x * 4 + z_from[k]]
            for j in NEAR:
                send(block, block, x_to[j], hx[p // 2][k])

    low = lax.broadcasted_iota(jnp.int32, (64, T), 1) < 64

    def place_back(h):
        for k, zc in ((3, z), (0, z_from[0]), (2, z_from[2]), (1, z_from[1])):
            wait(hx[h][k], back.at[0, pl.ds(0, 3)])
            for xc in range(4):
                j = xc * 4 + zc
                a, b = back_in[2 * h, j].astype(F32), back_in[2 * h + 1, j].astype(F32)
                back[h, j, 0:64] = jnp.where(low, a, pltpu.roll(b, 64, 1)).astype(BF16)
                back[h, j, 64:T] = jnp.where(low, pltpu.roll(a, 64, 1), b).astype(BF16)

    aggs, sents, biases = {}, {}, {}
    sums_x = {}
    sums_x[0] = x_total(0)
    total = rx_sum[...]
    wait(rz, rz_in)
    for k in range(3):
        total = total + rz_in[k]
    row_scale[...] = 1.0 / jnp.sqrt(1.0 + total)
    scales = []
    for h in range(2):
        turned = jnp.transpose(jnp.broadcast_to(row_scale[pl.ds(2 * z + h, 1), :], (T, T)))
        scales.append(jnp.concatenate([turned, turned], axis=1))
    for copy in held_in[3:]:
        copy.wait()

    def act(p):
        aggs[p], sents[p], biases[p] = activate(p, *sums_x[p])

    sums_x[2] = x_total(2)
    act(0)
    sums_x[1] = x_total(1)
    act(2)
    sums_x[3] = x_total(3)
    pass_on(0)
    act(1)
    pass_on(2)
    act(3)
    sent = jnp.concatenate([sents[p] for p in range(PIECES)], axis=0)
    agg = jnp.concatenate([aggs[p] for p in range(PIECES)], axis=0)
    turned = jnp.concatenate([jnp.transpose(agg[:T]), jnp.transpose(agg[T:])], axis=1)
    weight_term = split_dot(turned, sent)
    bias_term = jnp.broadcast_to((biases[0] + biases[1]) + (biases[2] + biases[3]), (8, 256))
    for c in range(2):
        for q in range(8):
            at = (q * 2 + c) * 8
            grads[c, q] = weight_term[at:at + 8]
        grads[c, 8] = bias_term
    gsib = group()
    send(grads.at[1 - core], gsib_in, sibling, gsib)
    pass_on(1)
    wait(gsib, gsib_in)
    for q in range(8):
        gq_buf[q, 0] = grads[core, q] + gsib_in[q]
        gq_buf[q, 1] = grads[core, 8] + gsib_in[8]
    gq_in[here] = gq_buf[here]
    gq = group()
    for k, (dz, dy) in enumerate(ROW_STEPS):
        there = ((zl + dz) % 2) * 4 + (y + dy) % 4
        send(gq_buf.at[there], gq_in.at[here], row_to[k], gq)
    pass_on(3)
    place_back(0)
    wait(gq, gq_in.at[pl.ds(0, far)])
    total = gq_in[0]
    for q in range(1, 8):
        total = total + gq_in[q]
    gz_buf[z] = total
    gz = group()
    for k in range(3):
        send(gz_buf.at[z], gz_buf.at[z], z_to[k], gz)
    place_back(1)

    def backward_term(p, rows):
        spots = [(lists[8, 2 * p + i], lists[9, 2 * p + i]) for i in range(2)]
        left = jnp.concatenate([back[r % 2, r // 2, rows, :] for _, r in spots], axis=1)
        right = jnp.concatenate([narrow[s] for s, _ in spots], axis=0)
        return jnp.dot(left, right, preferred_element_type=F32)

    near = [group(), group()]
    far_sends = [group(), group()]

    def put_col(i):
        for q in range(8):
            for h in range(2):
                t = q * 4 + (1 - core) * 2 + h
                col_part[i, q, h] = tile_sum(8, t, half(i)).astype(BF16)
        send(col_part.at[i], sib_in.at[i], sibling, near[i])

    def pair_up(i):
        wait(near[i], sib_in.at[i])
        for k, (dz, dy) in enumerate(ROW_STEPS):
            q = ((zl + dz) % 2) * 4 + (y + dy) % 4
            for h in range(2):
                own_part = tile_sum(8, q * 4 + core * 2 + h, half(i))
                pair[i, k, h] = (own_part + sib_in[i, q, h].astype(F32)).astype(BF16)
            send(pair.at[i, k], far_in.at[i, k], row_to[k], far_sends[i])

    products(8, backward_term, half(0), 0, PAIRS, nothing)
    put_col(0)
    acc = products(8, backward_term, half(1), 0, PAIRS // 3, nothing)
    pair_up(0)
    wait(gz, gz_buf.at[pl.ds(0, 3)])
    gx_buf[x] = (gz_buf[0] + gz_buf[1]) + (gz_buf[2] + gz_buf[3])
    gx = group()
    for k in range(3):
        send(gx_buf.at[x], gx_buf.at[x], x_to[k], gx)
    products(8, backward_term, half(1), PAIRS // 3, PAIRS, acc)
    put_col(1)
    wait(gx, gx_buf.at[pl.ds(0, 3)])
    total = ((gx_buf[0] + gx_buf[1]) + (gx_buf[2] + gx_buf[3])) * factor
    gall[here, core] = total[0]
    bias_out[...] = total[1, 0:1]
    mine = gall.at[here, core]
    ga = group()
    for device in row_to:
        send(mine, mine, device, ga)
    pair_up(1)
    blocks = [
        jnp.concatenate(
            [
                tile_sum(8, here * 4 + core * 2 + h, half(i)) + sib_in[i, here, h].astype(F32)
                for i in range(2)
            ],
            axis=0,
        )
        for h in range(2)
    ]
    wait(ga, gall.at[pl.ds(0, far), 0])
    held = gall.at[:, core]
    gs = group()
    send(held, held, sibling, gs)
    for i in range(2):
        wait(far_sends[i], far_in.at[i])
    for k in range(far):
        for h in range(2):
            both = jnp.concatenate([far_in[0, k, h], far_in[1, k, h]], axis=0)
            blocks[h] = blocks[h] + both.astype(F32)
    for h in range(2):
        block = blocks[h] * scale_keep[pl.ds(row * 2 + h, 1), :]
        feat_out[pl.ds(h * T, T), :] = jnp.transpose(block).astype(BF16)
    wait(gs, held)
    weight_out[...] = gall[...]
    links.drain()
    assert links.groups <= GROUPS


def emit_kernel(*refs):
    copies = [pltpu.make_async_copy(refs[k], refs[4 + k], refs[8].at[k]) for k in range(4)]
    for copy in copies:
        copy.start()
    for copy in copies:
        copy.wait()


def on_device(features, weight, bias, cotangent, tile_rows, tile_cols, tile_mask):
    nodes = features.shape[0] * lax.axis_size("row") * lax.axis_size("col")
    anywhere = pl.BlockSpec(memory_space=pl.ANY)
    vmem = pl.BlockSpec(memory_space=pltpu.VMEM)
    dma = pltpu.SemaphoreType.DMA
    shape = jax.ShapeDtypeStruct
    far = len(ROW_STEPS)
    outs = (
        shape((256, 256), BF16),
        shape((256, T), BF16),
        shape((8, 2, 8, 256), F32),
        shape((1, 256), F32),
    )
    results = pl.pallas_call(
        functools.partial(layer_kernel, 1.0 / float(nodes) ** 0.5),
        out_shape=tuple(pltpu.VMEM(out.shape, out.dtype) for out in outs),
        in_specs=[pl.BlockSpec(memory_space=pltpu.HBM)] * 7,
        out_specs=(vmem,) * 4,
        scratch_shapes=[
            pltpu.VMEM((T, 256), BF16),
            pltpu.VMEM((1, 256), F32),
            pltpu.VMEM((256, 256), BF16),
            pltpu.VMEM((1, SLOTS), jnp.int32),
            pltpu.VMEM((1, SLOTS), jnp.int32),
            pltpu.VMEM((SLOTS, T, T), jnp.int32),
            pltpu.VMEM((SLOTS + 1, T, T), BF16),
            pltpu.VMEM((PAIRS, T, T), F32),
            pltpu.VMEM((16, 256), jnp.int32),
            pltpu.VMEM((16, 256), jnp.int32),
            pltpu.SMEM((16, 256), jnp.int32),
            pltpu.VMEM((2, 8, 256, T), BF16),
            pltpu.VMEM((SLOTS, T), F32),
            pltpu.VMEM((32, T), F32),
            pltpu.VMEM((32, T), F32),
            pltpu.VMEM((32, T), F32),
            pltpu.VMEM((32, T), jnp.int16),
            pltpu.VMEM((far, 32, T), jnp.int16),
            pltpu.VMEM((4, 8, T), F32),
            pltpu.VMEM((3, 8, T), F32),
            pltpu.VMEM((8, T), F32),
            pltpu.VMEM((3, 8, T), F32),
            pltpu.VMEM((32, T, T), BF16),
            pltpu.VMEM((PIECES, 3, 4, PIECE, T), BF16),
            pltpu.VMEM((3, PIECES, 4, PIECE, T), BF16),
            pltpu.VMEM((PIECES, 3, PIECE, T), BF16),
            pltpu.VMEM((PIECES, 3, PIECE, T), BF16),
            pltpu.VMEM((PIECES, 16, PIECE, T), BF16),
            pltpu.VMEM((2, 16, T, T), BF16),
            pltpu.VMEM((32, T), F32),
            pltpu.VMEM((8, T), F32),
            pltpu.VMEM((2, 9, 8, 256), F32),
            pltpu.VMEM((9, 8, 256), F32),
            pltpu.VMEM((8, 2, 8, 256), F32),
            pltpu.VMEM((8, 2, 8, 256), F32),
            pltpu.VMEM((4, 2, 8, 256), F32),
            pltpu.VMEM((4, 2, 8, 256), F32),
            pltpu.VMEM((8, 2, 8, 256), F32),
            pltpu.VMEM((2, 8, 2, 64, T), BF16),
            pltpu.VMEM((2, 8, 2, 64, T), BF16),
            pltpu.VMEM((2, far, 2, 64, T), BF16),
            pltpu.VMEM((2, far, 2, 64, T), BF16),
            dma((SLOTS // CHUNK,)),
            dma,
            dma((6,)),
            dma((SENDS,)),
            dma((GROUPS,)),
        ],
        compiler_params=pltpu.CompilerParams(
            vmem_limit_bytes=VMEM_LIMIT, has_side_effects=True, collective_id=1
        ),
        name="layer",
    )(
        features,
        weight,
        bias.reshape(1, 256),
        cotangent,
        tile_rows.reshape(1, SLOTS),
        tile_cols.reshape(1, SLOTS),
        tile_mask.reshape(SLOTS, T, T),
    )
    activations, grad_features, grad_weight, grad_bias = pl.pallas_call(
        emit_kernel,
        out_shape=outs,
        in_specs=[vmem] * 4,
        out_specs=(anywhere,) * 4,
        scratch_shapes=[dma((4,))],
        name="emit",
    )(*(pltpu.with_memory_space_constraint(r, pltpu.VMEM) for r in results))
    return (activations, grad_features, grad_weight.reshape(T, 256), grad_bias.reshape(256))


def solution(mesh):
    placed = (
        P(("col", "row"), None),
        P(),
        P(),
        P(("row", "col"), None),
        P("row", "col", None),
        P("row", "col", None),
        P("row", "col", None, None, None),
    )
    return jax.shard_map(
        on_device,
        mesh=mesh,
        in_specs=placed,
        out_specs=(P(("row", "col"), None), P(("col", "row"), None), P(), P()),
        check_vma=False,
    )
```

```python
import functools

import jax
import jax.numpy as jnp
from jax import lax
from jax.experimental import pallas as pl
from jax.experimental.pallas import tpu as pltpu
from jax.sharding import PartitionSpec as P

F32 = jnp.float32
BF16 = jnp.bfloat16
T = 128
SLOTS = 160
CHUNK = 16
GROUP = 32
PAIRS = (SLOTS + 32) // 2
SENDS = 32
GROUPS = 54
VMEM_LIMIT = 56 * 1024 * 1024
ROW_STEPS = tuple((dz, dy) for dz in (1, 0) for dy in (2, 1, 3, 0) if (dz, dy) != (0, 0))
NEAR = (0, 2, 1)
PIECES = 4
PIECE = 256 // PIECES


class Links:
    def __init__(self, send_sems, recv_sems):
        self.send_sems, self.recv_sems = send_sems, recv_sems
        self.open, self.starts, self.groups = {}, 0, 0

    def group(self):
        self.groups += 1
        return self.groups - 1

    def send(self, src, dst, device, group):
        k = self.starts % SENDS
        self.starts += 1
        if k in self.open:
            self.open[k].wait_send()
        copy = pltpu.make_async_remote_copy(
            src_ref=src,
            dst_ref=dst,
            send_sem=self.send_sems.at[k],
            recv_sem=self.recv_sems.at[group],
            device_id=device,
            device_id_type=pl.DeviceIdType.MESH,
        )
        copy.start()
        self.open[k] = copy

    def wait(self, group, ruler):
        pltpu.make_async_copy(ruler, ruler, self.recv_sems.at[group]).wait()

    def drain(self):
        for copy in self.open.values():
            copy.wait_send()


def split_dot(a, b):
    hi = a.astype(BF16)
    lo = (a - hi.astype(F32)).astype(BF16)
    return jnp.dot(hi, b, preferred_element_type=F32) + jnp.dot(lo, b, preferred_element_type=F32)


def sort_lists(ids, others, lists, at):
    lane = lax.broadcasted_iota(jnp.int32, (1, 256), 1)
    key = (jnp.where(lane < SLOTS, ids, 64) * 256 + lane).astype(F32)
    along = jnp.broadcast_to(key, (256, 256))
    down = jnp.transpose(along)
    wide_lane = lax.broadcasted_iota(jnp.int32, (256, 256), 1).astype(F32)
    id_down = jnp.floor(down * (1.0 / 256.0))
    rank = jnp.sum((along < down).astype(F32), axis=1, keepdims=True)
    held = jnp.sum((id_down == wide_lane).astype(F32), axis=0, keepdims=True)
    odd = held - 2.0 * jnp.floor(held * 0.5)
    below = jnp.sum(jnp.where(wide_lane < id_down, odd, 0.0), axis=1, keepdims=True)
    pos = rank + below
    first = 1.0 - (pos - 2.0 * jnp.floor(pos * 0.5))
    place = jnp.where(id_down < 63.0, (pos == wide_lane).astype(F32), 0.0).astype(BF16)
    row = lax.broadcasted_iota(jnp.int32, (8, 256), 0)
    values = jnp.where(row == 0, lane + 1, jnp.where(row == 1, others, ids))
    moved = jnp.dot(values.astype(F32).astype(BF16), place, preferred_element_type=F32)
    upto = jnp.where(id_down <= wide_lane, first, 0.0)
    last = jnp.sum(upto, axis=0, keepdims=True) - 1.0
    found = jnp.where(row == 3, last, moved).astype(jnp.int32)
    least = jnp.where(row == 3, -1, 0)
    most = jnp.where(row == 0, SLOTS, jnp.where(row == 3, PAIRS - 1, 31))
    lists[pl.ds(at, 8), :] = jnp.minimum(jnp.maximum(found, least), most)


def layer_kernel(
    factor,
    feat, weight_hbm, bias_hbm, cot_hbm, row_hbm, col_hbm, mask,
    act_out, feat_out, weight_out, bias_out,
    weight, bias, cot, row_ids, col_ids,
    mask_in, narrow, running, padded, lists_v, lists,
    feats, sums, count, sib_count, pair_count, pair_send, far_count,
    row_count, rx_in, rx_sum, rz_in, scaled,
    part, x_in, z_buf, z_in, back_in, back,
    scale_keep, row_scale, grads, gsib_in, gq_buf, gq_in, gx_buf, gz_buf, gall,
    col_part, sib_in, pair, far_in,
    mask_sem, list_sem, in_sem, send_sems, recv_sems,
):
    row, col = lax.axis_index("row"), lax.axis_index("col")
    zl, y, core = row // 8, (row // 2) % 4, row % 2
    x, z = col // 4, col % 4
    here = zl * 4 + y
    sibling = (zl * 8 + y * 2 + 1 - core, col)
    row_to = [(((zl + dz) % 2) * 8 + ((y + dy) % 4) * 2 + core, col) for dz, dy in ROW_STEPS]
    row_from = [((zl - dz + 2) % 2) * 4 + (y - dy + 4) % 4 for dz, dy in ROW_STEPS]
    far = len(ROW_STEPS)
    x_at = [(x + d) % 4 for d in (1, 2, 3)]
    z_at = [(z + d) % 4 for d in (1, 2, 3)]
    x_to = [(row, p * 4 + z) for p in x_at]
    z_to = [(row, x * 4 + p) for p in z_at]
    x_from = [(x - d + 4) % 4 for d in (1, 2, 3)]
    z_from = [(z - d + 4) % 4 for d in (1, 2, 3)]
    links = Links(send_sems, recv_sems)
    send, wait, group = links.send, links.wait, links.group

    barrier = pltpu.get_barrier_semaphore()
    peers = [sibling] + row_to + x_to + z_to
    for device in peers:
        pl.semaphore_signal(
            barrier, inc=1, device_id=device, device_id_type=pl.DeviceIdType.MESH
        )
    chunks = SLOTS // CHUNK
    loads = []
    held_in = []
    for k, (src, dst) in enumerate(
        (
            (row_hbm, row_ids),
            (col_hbm, col_ids),
            (feat, feats.at[core, here]),
            (weight_hbm, weight),
            (bias_hbm, bias),
            (cot_hbm, cot),
        )
    ):
        held_in.append(pltpu.make_async_copy(src, dst, in_sem.at[k]))
    for copy in held_in[:2]:
        copy.start()
    for c in range(chunks):
        span = pl.ds(c * CHUNK, CHUNK)
        load = pltpu.make_async_copy(mask.at[span], mask_in.at[span], mask_sem.at[c])
        load.start()
        loads.append(load)
        if c == 1:
            for copy in held_in[2:]:
                copy.start()

    narrow[0] = jnp.zeros((T, T), BF16)

    def take(c):
        loads[c].wait()

        def eight(g, carry):
            at = pl.multiple_of(c * CHUNK + g * 8, 8)
            wide = mask_in[pl.ds(at, 8)].astype(F32)
            narrow[pl.ds(at + 1, 8)] = wide.astype(BF16)
            sums[pl.ds(at, 8), :] = jnp.sum(wide, axis=1)
            return carry

        lax.fori_loop(0, CHUNK // 8, eight, 0)

    for c in range(chunks // 2):
        take(c)
    pl.semaphore_wait(barrier, len(peers))
    held_in[2].wait()
    mine = feats.at[core, here]
    own = [group() for _ in range(far + 1)]
    for k in (0, 1, 2, 3, 4, far):
        send(mine, mine, (row_to + [sibling])[k], own[k])
    for c in range(chunks // 2, chunks):
        take(c)
    slot_row = lax.broadcasted_iota(jnp.int32, (32, SLOTS), 0)
    for copy in held_in[:2]:
        copy.wait()
    onehot = (slot_row == col_ids[...]).astype(BF16)
    count[...] = jnp.dot(onehot, sums[...].astype(BF16), preferred_element_type=F32)
    near_count = group()
    send(count, sib_count, sibling, near_count)

    wait(near_count, sib_count)
    pair_count[...] = count[...] + sib_count[...]
    pair_send[...] = (pair_count[...].astype(jnp.int32) - SLOTS * T).astype(jnp.int16)
    far_counts = group()
    for k in range(far):
        send(pair_send, far_count.at[k], row_to[k], far_counts)
    for k in (5, 6):
        send(mine, mine, row_to[k], own[k])
    padded[...] = jnp.zeros_like(padded)
    padded[0:1, 0:SLOTS] = row_ids[...]
    padded[8:9, 0:SLOTS] = col_ids[...]
    rows_wide, cols_wide = padded[0:1, :], padded[8:9, :]
    sort_lists(rows_wide, cols_wide, lists_v, 0)
    sort_lists(cols_wide, rows_wide, lists_v, 8)
    list_copy = pltpu.make_async_copy(lists_v, lists, list_sem)
    list_copy.start()
    ones = jnp.ones((8, T), BF16)

    def row_sums(g, carry):
        at = pl.multiple_of(g * 8, 8)
        tiles = narrow[pl.ds(at + 1, 8)].reshape(8 * T, T)
        got = lax.dot_general(ones, tiles, (((1,), (1,)), ((), ())), preferred_element_type=F32)
        sums[pl.ds(at, 8), :] = jnp.concatenate(
            [got[0:1, i * T:(i + 1) * T] for i in range(8)], axis=0
        )
        return carry

    lax.fori_loop(0, SLOTS // 8, row_sums, 0)
    onehot = (slot_row == row_ids[...]).astype(BF16)
    got = jnp.dot(onehot, sums[...].astype(BF16), preferred_element_type=F32)
    for c in range(4):
        row_count[c] = got[c * 8:c * 8 + 8]
    rx = group()
    for k in range(3):
        send(row_count.at[x_at[k]], rx_in.at[k], x_to[k], rx)
    forwards = group()
    for k in range(far):
        wait(own[k], feats.at[0, 0])
        block = feats.at[core, row_from[k]]
        send(block, block, sibling, forwards)
    total = pair_count[...]
    wait(far_counts, far_count)
    for k in range(far):
        total = total + (far_count[k].astype(jnp.int32) + SLOTS * T).astype(F32)
    scale_keep[...] = 1.0 / jnp.sqrt(1.0 + total)
    parts = [
        scale_keep[pl.ds((q * 2 + c) * 2, 2), :] for c in (core, 1 - core) for q in range(8)
    ]
    turned = jnp.transpose(jnp.concatenate(parts + [jnp.zeros((96, T), F32)], axis=0))

    def scale_tiles(c, at):
        for q in range(8):
            for h in range(2):
                block = feats[c, q, pl.ds(h * T, T), :].astype(F32)
                lane = at + q * 2 + h
                scaled[(q * 2 + c) * 2 + h] = (block * turned[:, lane:lane + 1]).astype(BF16)

    scale_tiles(core, 0)
    wait(own[far], feats.at[0, 0])
    wait(forwards, feats.at[0, pl.ds(0, far)])
    scale_tiles(1 - core, 16)
    list_copy.wait()

    def half(i):
        return pl.ds(i * 64, 64)

    def products(at, term, rows, begin, end, acc):
        def group_of(g, acc):
            terms = [term(g * GROUP + i, rows) for i in range(GROUP)]
            for i in range(GROUP):
                p = g * GROUP + i
                same = lists[at + 2, 2 * p] == lists[at + 2, 2 * jnp.maximum(p - 1, 0)]
                acc = jnp.where(same, acc, 0.0) + terms[i]
                running[p, rows, :] = acc
            return acc

        return lax.fori_loop(begin // GROUP, end // GROUP, group_of, acc)

    def tile_sum(at, t, rows=pl.ds(0, T)):
        last = lists[at + 3, t]
        before = jnp.where(t > 0, lists[at + 3, jnp.maximum(t - 1, 0)], -1)
        return jnp.where(last > before, running[jnp.maximum(last, 0), rows, :], 0.0)

    def piece_sum(p, chunk):
        return tile_sum(0, chunk * 2 + p // 2, pl.ds(p % 2 * PIECE, PIECE))

    def forward_term(p, rows):
        spots = [(lists[0, 2 * p + i], lists[1, 2 * p + i]) for i in range(2)]
        left = jnp.concatenate([narrow[s, rows, :] for s, _ in spots], axis=1)
        right = jnp.concatenate([scaled[c] for _, c in spots], axis=0)
        return jnp.dot(left, right, preferred_element_type=F32)

    x_sends = [group() for _ in range(PIECES)]
    nothing = jnp.zeros((64, T), F32)
    for i in range(2):

        products(0, forward_term, half(i), 0, PAIRS, nothing)

        for p in (i, i + 2):
            for k in NEAR:
                for zc in range(4):
                    part[p, k, zc] = piece_sum(p, x_at[k] * 4 + zc).astype(BF16)
                send(part.at[p, k], x_in.at[k, p], x_to[k], x_sends[p])

    total = row_count[x]
    wait(rx, rx_in)
    for k in range(3):
        total = total + rx_in[k]
    rx_sum[...] = total
    rz = group()
    for k in range(3):
        send(rx_sum, rz_in.at[k], z_to[k], rz)

    def x_total(p):
        wait(x_sends[p], back.at[pl.ds(0, 6)])
        z_sends = group()
        for e in (2, 1, 3, 0):
            zc = z if e == 0 else z_at[e - 1]
            total = piece_sum(p, x * 4 + zc)
            for k in range(3):
                total = total + x_in[k, p, zc].astype(F32)
            if e:
                z_buf[p, e - 1] = total.astype(BF16)
                send(z_buf.at[p, e - 1], z_in.at[p, e - 1], z_to[e - 1], z_sends)
        return total, z_sends

    def activate(p, total, z_sends):
        wait(z_sends, z_in.at[p])
        for k in range(3):
            total = total + z_in[p, k].astype(F32)
        span = pl.ds(p * PIECE, PIECE)
        scale = scales[p // 2][p % 2 * PIECE:p % 2 * PIECE + PIECE]
        pre = scale * split_dot(total, weight[...]) + bias[...]
        sig = jax.nn.sigmoid(pre)
        act_out[span, :] = (pre * sig).astype(BF16)
        grad_pre = cot[span, :].astype(F32) * sig * (1.0 + pre * (1.0 - sig))
        sent = (scale * grad_pre).astype(BF16)
        turned = lax.dot_general(
            weight[...], sent, (((1,), (1,)), ((), ())), preferred_element_type=F32
        )
        back_in[p, col] = jnp.concatenate([turned[:64], turned[64:]], axis=1).astype(BF16)
        mine = back_in.at[p, col]
        for k in (1, 0, 2):
            send(mine, mine, z_to[k], hz[p][k])
        for k in NEAR:
            send(mine, mine, x_to[k], hx[p // 2][3])
        return total, sent, jnp.sum(grad_pre, axis=0, keepdims=True)

    hz = [[group() for _ in range(3)] for _ in range(PIECES)]
    hx = [[group() for _ in range(4)] for _ in range(2)]

    def pass_on(p):
        for k in (0, 2, 1):
            wait(hz[p][k], z_in.at[0, 0])
            block = back_in.at[p, x * 4 + z_from[k]]
            for j in NEAR:
                send(block, block, x_to[j], hx[p // 2][k])

    low = lax.broadcasted_iota(jnp.int32, (64, T), 1) < 64

    def place_back(h):
        for k, zc in ((3, z), (0, z_from[0]), (2, z_from[2]), (1, z_from[1])):
            wait(hx[h][k], back.at[pl.ds(0, 3)])
            for xc in range(4):
                j = xc * 4 + zc
                a, b = back_in[2 * h, j].astype(F32), back_in[2 * h + 1, j].astype(F32)
                back[j * 2 + h, 0:64] = jnp.where(low, a, pltpu.roll(b, 64, 1)).astype(BF16)
                back[j * 2 + h, 64:T] = jnp.where(low, pltpu.roll(a, 64, 1), b).astype(BF16)

    aggs, sents, biases = {}, {}, {}
    sums_x = {}
    sums_x[0] = x_total(0)
    total = rx_sum[...]
    wait(rz, rz_in)
    for k in range(3):
        total = total + rz_in[k]
    row_scale[...] = 1.0 / jnp.sqrt(1.0 + total)
    scales = []
    for h in range(2):
        turned = jnp.transpose(jnp.broadcast_to(row_scale[pl.ds(2 * z + h, 1), :], (T, T)))
        scales.append(jnp.concatenate([turned, turned], axis=1))
    for copy in held_in[3:]:
        copy.wait()

    def act(p):
        aggs[p], sents[p], biases[p] = activate(p, *sums_x[p])

    sums_x[2] = x_total(2)
    act(0)
    sums_x[1] = x_total(1)
    act(2)
    sums_x[3] = x_total(3)
    pass_on(0)
    act(1)
    pass_on(2)
    act(3)
    sent = jnp.concatenate([sents[p] for p in range(PIECES)], axis=0)
    agg = jnp.concatenate([aggs[p] for p in range(PIECES)], axis=0)
    turned = jnp.concatenate([jnp.transpose(agg[:T]), jnp.transpose(agg[T:])], axis=1)
    weight_term = split_dot(turned, sent)
    bias_term = jnp.broadcast_to((biases[0] + biases[1]) + (biases[2] + biases[3]), (8, 256))
    for c in range(2):
        for q in range(8):
            at = (q * 2 + c) * 8
            grads[c, q] = weight_term[at:at + 8]
        grads[c, 8] = bias_term
    gsib = group()
    send(grads.at[1 - core], gsib_in, sibling, gsib)
    pass_on(1)
    wait(gsib, gsib_in)
    for q in range(8):
        gq_buf[q, 0] = grads[core, q] + gsib_in[q]
        gq_buf[q, 1] = grads[core, 8] + gsib_in[8]
    gq_in[here] = gq_buf[here]
    gq = group()
    for k, (dz, dy) in enumerate(ROW_STEPS):
        there = ((zl + dz) % 2) * 4 + (y + dy) % 4
        send(gq_buf.at[there], gq_in.at[here], row_to[k], gq)
    pass_on(3)
    wait(gq, gq_in.at[pl.ds(0, far)])
    total = gq_in[0]
    for q in range(1, 8):
        total = total + gq_in[q]
    gz_buf[z] = total
    gz = group()
    for k in range(3):
        send(gz_buf.at[z], gz_buf.at[z], z_to[k], gz)
    place_back(0)
    place_back(1)

    def backward_term(p, rows):
        spots = [(lists[8, 2 * p + i], lists[9, 2 * p + i]) for i in range(2)]
        left = jnp.concatenate([back[r, rows, :] for _, r in spots], axis=1)
        right = jnp.concatenate([narrow[s] for s, _ in spots], axis=0)
        return jnp.dot(left, right, preferred_element_type=F32)

    near = [group(), group()]
    far_sends = [group(), group()]

    def put_col(i):
        for q in range(8):
            for h in range(2):
                t = q * 4 + (1 - core) * 2 + h
                col_part[i, q, h] = tile_sum(8, t, half(i)).astype(BF16)
        send(col_part.at[i], sib_in.at[i], sibling, near[i])

    def pair_up(i):
        wait(near[i], sib_in.at[i])
        for k, (dz, dy) in enumerate(ROW_STEPS):
            q = ((zl + dz) % 2) * 4 + (y + dy) % 4
            for h in range(2):
                own_part = tile_sum(8, q * 4 + core * 2 + h, half(i))
                pair[i, k, h] = (own_part + sib_in[i, q, h].astype(F32)).astype(BF16)
            send(pair.at[i, k], far_in.at[i, k], row_to[k], far_sends[i])

    products(8, backward_term, half(0), 0, PAIRS, nothing)
    put_col(0)
    acc = products(8, backward_term, half(1), 0, PAIRS // 3, nothing)
    wait(gz, gz_buf.at[pl.ds(0, 3)])
    gx_buf[x] = (gz_buf[0] + gz_buf[1]) + (gz_buf[2] + gz_buf[3])
    gx = group()
    for k in range(3):
        send(gx_buf.at[x], gx_buf.at[x], x_to[k], gx)
    pair_up(0)
    products(8, backward_term, half(1), PAIRS // 3, PAIRS, acc)
    put_col(1)
    wait(gx, gx_buf.at[pl.ds(0, 3)])
    total = ((gx_buf[0] + gx_buf[1]) + (gx_buf[2] + gx_buf[3])) * factor
    gall[here, core] = total[0]
    bias_out[...] = total[1, 0:1]
    mine = gall.at[here, core]
    ga = group()
    for device in row_to:
        send(mine, mine, device, ga)
    pair_up(1)
    blocks = [
        jnp.concatenate(
            [
                tile_sum(8, here * 4 + core * 2 + h, half(i)) + sib_in[i, here, h].astype(F32)
                for i in range(2)
            ],
            axis=0,
        )
        for h in range(2)
    ]
    wait(ga, gall.at[pl.ds(0, far), 0])
    held = gall.at[:, core]
    gs = group()
    send(held, held, sibling, gs)
    for i in range(2):
        wait(far_sends[i], far_in.at[i])
    for k in range(far):
        for h in range(2):
            both = jnp.concatenate([far_in[0, k, h], far_in[1, k, h]], axis=0)
            blocks[h] = blocks[h] + both.astype(F32)
    for h in range(2):
        block = blocks[h] * scale_keep[pl.ds(row * 2 + h, 1), :]
        feat_out[pl.ds(h * T, T), :] = jnp.transpose(block).astype(BF16)
    wait(gs, held)
    weight_out[...] = gall[...]
    links.drain()
    assert links.groups <= GROUPS


def emit_kernel(*refs):
    copies = [pltpu.make_async_copy(refs[k], refs[4 + k], refs[8].at[k]) for k in range(4)]
    for copy in copies:
        copy.start()
    for copy in copies:
        copy.wait()


def on_device(features, weight, bias, cotangent, tile_rows, tile_cols, tile_mask):
    nodes = features.shape[0] * lax.axis_size("row") * lax.axis_size("col")
    anywhere = pl.BlockSpec(memory_space=pl.ANY)
    vmem = pl.BlockSpec(memory_space=pltpu.VMEM)
    dma = pltpu.SemaphoreType.DMA
    shape = jax.ShapeDtypeStruct
    far = len(ROW_STEPS)
    outs = (
        shape((256, 256), BF16),
        shape((256, T), BF16),
        shape((8, 2, 8, 256), F32),
        shape((1, 256), F32),
    )
    results = pl.pallas_call(
        functools.partial(layer_kernel, 1.0 / float(nodes) ** 0.5),
        out_shape=tuple(pltpu.VMEM(out.shape, out.dtype) for out in outs),
        in_specs=[pl.BlockSpec(memory_space=pltpu.HBM)] * 7,
        out_specs=(vmem,) * 4,
        scratch_shapes=[
            pltpu.VMEM((T, 256), BF16),
            pltpu.VMEM((1, 256), F32),
            pltpu.VMEM((256, 256), BF16),
            pltpu.VMEM((1, SLOTS), jnp.int32),
            pltpu.VMEM((1, SLOTS), jnp.int32),
            pltpu.VMEM((SLOTS, T, T), jnp.int32),
            pltpu.VMEM((SLOTS + 1, T, T), BF16),
            pltpu.VMEM((PAIRS, T, T), F32),
            pltpu.VMEM((16, 256), jnp.int32),
            pltpu.VMEM((16, 256), jnp.int32),
            pltpu.SMEM((16, 256), jnp.int32),
            pltpu.VMEM((2, 8, 256, T), BF16),
            pltpu.VMEM((SLOTS, T), F32),
            pltpu.VMEM((32, T), F32),
            pltpu.VMEM((32, T), F32),
            pltpu.VMEM((32, T), F32),
            pltpu.VMEM((32, T), jnp.int16),
            pltpu.VMEM((far, 32, T), jnp.int16),
            pltpu.VMEM((4, 8, T), F32),
            pltpu.VMEM((3, 8, T), F32),
            pltpu.VMEM((8, T), F32),
            pltpu.VMEM((3, 8, T), F32),
            pltpu.VMEM((32, T, T), BF16),
            pltpu.VMEM((PIECES, 3, 4, PIECE, T), BF16),
            pltpu.VMEM((3, PIECES, 4, PIECE, T), BF16),
            pltpu.VMEM((PIECES, 3, PIECE, T), BF16),
            pltpu.VMEM((PIECES, 3, PIECE, T), BF16),
            pltpu.VMEM((PIECES, 16, PIECE, T), BF16),
            pltpu.VMEM((32, T, T), BF16),
            pltpu.VMEM((32, T), F32),
            pltpu.VMEM((8, T), F32),
            pltpu.VMEM((2, 9, 8, 256), F32),
            pltpu.VMEM((9, 8, 256), F32),
            pltpu.VMEM((8, 2, 8, 256), F32),
            pltpu.VMEM((8, 2, 8, 256), F32),
            pltpu.VMEM((4, 2, 8, 256), F32),
            pltpu.VMEM((4, 2, 8, 256), F32),
            pltpu.VMEM((8, 2, 8, 256), F32),
            pltpu.VMEM((2, 8, 2, 64, T), BF16),
            pltpu.VMEM((2, 8, 2, 64, T), BF16),
            pltpu.VMEM((2, far, 2, 64, T), BF16),
            pltpu.VMEM((2, far, 2, 64, T), BF16),
            dma((SLOTS // CHUNK,)),
            dma,
            dma((6,)),
            dma((SENDS,)),
            dma((GROUPS,)),
        ],
        compiler_params=pltpu.CompilerParams(
            vmem_limit_bytes=VMEM_LIMIT, has_side_effects=True, collective_id=1
        ),
        name="layer",
    )(
        features,
        weight,
        bias.reshape(1, 256),
        cotangent,
        tile_rows.reshape(1, SLOTS),
        tile_cols.reshape(1, SLOTS),
        tile_mask.reshape(SLOTS, T, T),
    )
    activations, grad_features, grad_weight, grad_bias = pl.pallas_call(
        emit_kernel,
        out_shape=outs,
        in_specs=[vmem] * 4,
        out_specs=(anywhere,) * 4,
        scratch_shapes=[dma((4,))],
        name="emit",
    )(*(pltpu.with_memory_space_constraint(r, pltpu.VMEM) for r in results))
    return (activations, grad_features, grad_weight.reshape(T, 256), grad_bias.reshape(256))


def solution(mesh):
    placed = (
        P(("col", "row"), None),
        P(),
        P(),
        P(("row", "col"), None),
        P("row", "col", None),
        P("row", "col", None),
        P("row", "col", None, None, None),
    )
    return jax.shard_map(
        on_device,
        mesh=mesh,
        in_specs=placed,
        out_specs=(P(("row", "col"), None), P(("col", "row"), None), P(), P()),
        check_vma=False,
    )
```

```python
import functools

import jax
import jax.numpy as jnp
from jax import lax
from jax.experimental import pallas as pl
from jax.experimental.pallas import tpu as pltpu
from jax.sharding import PartitionSpec as P

F32 = jnp.float32
BF16 = jnp.bfloat16
T = 128
SLOTS = 160
CHUNK = 32
GROUP = 32
PAIRS = (SLOTS + 32) // 2
SENDS = 24
GROUPS = 55
VMEM_LIMIT = 56 * 1024 * 1024
ROW_STEPS = tuple((dz, dy) for dz in (1, 0) for dy in (2, 1, 3, 0) if (dz, dy) != (0, 0))
NEAR = (0, 2, 1)
PIECES = 4
PIECE = 256 // PIECES


class Links:
    def __init__(self, send_sems, recv_sems):
        self.send_sems, self.recv_sems = send_sems, recv_sems
        self.open, self.starts, self.groups = {}, 0, 0

    def group(self):
        self.groups += 1
        return self.groups - 1

    def send(self, src, dst, device, group):
        k = self.starts % SENDS
        self.starts += 1
        if k in self.open:
            self.open[k].wait_send()
        copy = pltpu.make_async_remote_copy(
            src_ref=src,
            dst_ref=dst,
            send_sem=self.send_sems.at[k],
            recv_sem=self.recv_sems.at[group],
            device_id=device,
            device_id_type=pl.DeviceIdType.MESH,
        )
        copy.start()
        self.open[k] = copy

    def wait(self, group, ruler):
        pltpu.make_async_copy(ruler, ruler, self.recv_sems.at[group]).wait()

    def drain(self):
        for copy in self.open.values():
            copy.wait_send()


def split_dot(a, b):
    hi = a.astype(BF16)
    lo = (a - hi.astype(F32)).astype(BF16)
    return jnp.dot(hi, b, preferred_element_type=F32) + jnp.dot(lo, b, preferred_element_type=F32)


def sort_lists(ids, others, lists, at):
    lane = lax.broadcasted_iota(jnp.int32, (1, 256), 1)
    key = (jnp.where(lane < SLOTS, ids, 64) * 256 + lane).astype(F32)
    along = jnp.broadcast_to(key, (256, 256))
    down = jnp.transpose(along)
    wide_lane = lax.broadcasted_iota(jnp.int32, (256, 256), 1).astype(F32)
    id_down = jnp.floor(down * (1.0 / 256.0))
    rank = jnp.sum((along < down).astype(F32), axis=1, keepdims=True)
    held = jnp.sum((id_down == wide_lane).astype(F32), axis=0, keepdims=True)
    odd = held - 2.0 * jnp.floor(held * 0.5)
    below = jnp.sum(jnp.where(wide_lane < id_down, odd, 0.0), axis=1, keepdims=True)
    pos = rank + below
    first = 1.0 - (pos - 2.0 * jnp.floor(pos * 0.5))
    place = jnp.where(id_down < 63.0, (pos == wide_lane).astype(F32), 0.0).astype(BF16)
    row = lax.broadcasted_iota(jnp.int32, (8, 256), 0)
    values = jnp.where(row == 0, lane + 1, jnp.where(row == 1, others, ids))
    moved = jnp.dot(values.astype(F32).astype(BF16), place, preferred_element_type=F32)
    upto = jnp.where(id_down <= wide_lane, first, 0.0)
    last = jnp.sum(upto, axis=0, keepdims=True) - 1.0
    found = jnp.where(row == 3, last, moved).astype(jnp.int32)
    least = jnp.where(row == 3, -1, 0)
    most = jnp.where(row == 0, SLOTS, jnp.where(row == 3, PAIRS - 1, 31))
    lists[pl.ds(at, 8), :] = jnp.minimum(jnp.maximum(found, least), most)


def layer_kernel(
    factor,
    feat, weight_hbm, bias_hbm, cot_hbm, row_hbm, col_hbm, mask,
    act_out, feat_out, weight_out, bias_out,
    weight, bias, cot, row_ids, col_ids,
    mask_in, narrow, running, padded, lists_v, lists,
    feats, sums, count, sib_count, pair_count, pair_send, far_count,
    row_count, rx_in, rx_sum, rz_in, scaled,
    part, x_in, z_buf, z_in, back_in, back,
    scale_keep, row_scale, grads, gsib_in, gq_buf, gq_in, gx_buf, gz_buf, gall,
    col_part, sib_in, pair, far_in,
    mask_sem, list_sem, in_sem, send_sems, recv_sems,
):
    row, col = lax.axis_index("row"), lax.axis_index("col")
    zl, y, core = row // 8, (row // 2) % 4, row % 2
    x, z = col // 4, col % 4
    here = zl * 4 + y
    sibling = (zl * 8 + y * 2 + 1 - core, col)
    row_to = [(((zl + dz) % 2) * 8 + ((y + dy) % 4) * 2 + core, col) for dz, dy in ROW_STEPS]
    row_from = [((zl - dz + 2) % 2) * 4 + (y - dy + 4) % 4 for dz, dy in ROW_STEPS]
    far = len(ROW_STEPS)
    x_at = [(x + d) % 4 for d in (1, 2, 3)]
    z_at = [(z + d) % 4 for d in (1, 2, 3)]
    x_to = [(row, p * 4 + z) for p in x_at]
    z_to = [(row, x * 4 + p) for p in z_at]
    x_from = [(x - d + 4) % 4 for d in (1, 2, 3)]
    z_from = [(z - d + 4) % 4 for d in (1, 2, 3)]
    links = Links(send_sems, recv_sems)
    send, wait, group = links.send, links.wait, links.group

    barrier = pltpu.get_barrier_semaphore()
    peers = [sibling] + row_to + x_to + z_to
    for device in peers:
        pl.semaphore_signal(
            barrier, inc=1, device_id=device, device_id_type=pl.DeviceIdType.MESH
        )
    chunks = SLOTS // CHUNK
    loads = []
    held_in = []
    for k, (src, dst) in enumerate(
        (
            (row_hbm, row_ids),
            (col_hbm, col_ids),
            (feat, feats.at[core, here]),
            (weight_hbm, weight),
            (bias_hbm, bias),
            (cot_hbm, cot),
        )
    ):
        held_in.append(pltpu.make_async_copy(src, dst, in_sem.at[k]))
    for copy in held_in[:2]:
        copy.start()
    for c in range(chunks):
        span = pl.ds(c * CHUNK, CHUNK)
        load = pltpu.make_async_copy(mask.at[span], mask_in.at[span], mask_sem.at[c])
        load.start()
        loads.append(load)
        if c == 1:
            for copy in held_in[2:]:
                copy.start()

    narrow[0] = jnp.zeros((T, T), BF16)

    def take(c):
        loads[c].wait()

        def eight(g, carry):
            at = pl.multiple_of(c * CHUNK + g * 8, 8)
            wide = mask_in[pl.ds(at, 8)].astype(F32)
            narrow[pl.ds(at + 1, 8)] = wide.astype(BF16)
            sums[pl.ds(at, 8), :] = jnp.sum(wide, axis=1)
            return carry

        lax.fori_loop(0, CHUNK // 8, eight, 0)

    for c in range(chunks // 2 + 1):
        take(c)
    pl.semaphore_wait(barrier, len(peers))
    held_in[2].wait()
    mine = feats.at[core, here]
    own = [group() for _ in range(far + 1)]
    for k in (0, 1, 2, 3, 4, far):
        send(mine, mine, (row_to + [sibling])[k], own[k])
    for c in range(chunks // 2 + 1, chunks):
        take(c)
    slot_row = lax.broadcasted_iota(jnp.int32, (32, SLOTS), 0)
    for copy in held_in[:2]:
        copy.wait()
    onehot = (slot_row == col_ids[...]).astype(BF16)
    count[...] = jnp.dot(onehot, sums[...].astype(BF16), preferred_element_type=F32)
    near_count = group()
    send(count, sib_count, sibling, near_count)

    wait(near_count, sib_count)
    pair_count[...] = count[...] + sib_count[...]
    pair_send[...] = (pair_count[...].astype(jnp.int32) - SLOTS * T).astype(jnp.int16)
    far_counts = group()
    for k in range(far):
        send(pair_send, far_count.at[k], row_to[k], far_counts)
    for k in (5, 6):
        send(mine, mine, row_to[k], own[k])
    padded[...] = jnp.zeros_like(padded)
    padded[0:1, 0:SLOTS] = row_ids[...]
    padded[8:9, 0:SLOTS] = col_ids[...]
    rows_wide, cols_wide = padded[0:1, :], padded[8:9, :]
    sort_lists(rows_wide, cols_wide, lists_v, 0)
    sort_lists(cols_wide, rows_wide, lists_v, 8)
    list_copy = pltpu.make_async_copy(lists_v, lists, list_sem)
    list_copy.start()
    ones = jnp.ones((8, T), BF16)

    def row_sums(g, carry):
        at = pl.multiple_of(g * 8, 8)
        tiles = narrow[pl.ds(at + 1, 8)].reshape(8 * T, T)
        got = lax.dot_general(ones, tiles, (((1,), (1,)), ((), ())), preferred_element_type=F32)
        sums[pl.ds(at, 8), :] = jnp.concatenate(
            [got[0:1, i * T:(i + 1) * T] for i in range(8)], axis=0
        )
        return carry

    lax.fori_loop(0, SLOTS // 8, row_sums, 0)
    onehot = (slot_row == row_ids[...]).astype(BF16)
    got = jnp.dot(onehot, sums[...].astype(BF16), preferred_element_type=F32)
    for c in range(4):
        row_count[c] = got[c * 8:c * 8 + 8]
    rx = group()
    for k in range(3):
        send(row_count.at[x_at[k]], rx_in.at[k], x_to[k], rx)
    forwards = [group(), group()]

    def forward_block(k):
        wait(own[k], feats.at[0, 0])
        block = feats.at[core, row_from[k]]
        send(block, block, sibling, forwards[k // 5])

    for k in range(5):
        forward_block(k)
    total = pair_count[...]
    wait(far_counts, far_count)
    for k in range(far):
        total = total + (far_count[k].astype(jnp.int32) + SLOTS * T).astype(F32)
    scale_keep[...] = 1.0 / jnp.sqrt(1.0 + total)
    order = row_from + [here]
    parts = [scale_keep[pl.ds((q * 2 + c) * 2, 2), :] for c in (core, 1 - core) for q in order]
    turned = jnp.transpose(jnp.concatenate(parts + [jnp.zeros((96, T), F32)], axis=0))

    def scale_block(side, k):
        c, q = (core, 1 - core)[side], order[k]
        for h in range(2):
            lane = side * 16 + k * 2 + h
            block = feats[c, q, pl.ds(h * T, T), :].astype(F32)
            scaled[(q * 2 + c) * 2 + h] = (block * turned[:, lane:lane + 1]).astype(BF16)

    for k in (far, 0, 1, 2, 3, 4):
        scale_block(0, k)
    for k in (5, 6):
        forward_block(k)
    scale_block(0, 5)
    scale_block(0, 6)
    wait(own[far], feats.at[0, 0])
    scale_block(1, far)
    wait(forwards[0], feats.at[0, pl.ds(0, 5)])
    for k in range(5):
        scale_block(1, k)
    wait(forwards[1], feats.at[0, pl.ds(0, 2)])
    scale_block(1, 5)
    scale_block(1, 6)
    list_copy.wait()

    def half(i):
        return pl.ds(i * 64, 64)

    def products(at, term, rows, begin, end, acc):
        def group_of(g, acc):
            terms = [term(g * GROUP + i, rows) for i in range(GROUP)]
            for i in range(GROUP):
                p = g * GROUP + i
                same = lists[at + 2, 2 * p] == lists[at + 2, 2 * jnp.maximum(p - 1, 0)]
                acc = jnp.where(same, acc, 0.0) + terms[i]
                running[p, rows, :] = acc
            return acc

        return lax.fori_loop(begin // GROUP, end // GROUP, group_of, acc)

    def tile_sum(at, t, rows=pl.ds(0, T)):
        last = lists[at + 3, t]
        before = jnp.where(t > 0, lists[at + 3, jnp.maximum(t - 1, 0)], -1)
        return jnp.where(last > before, running[jnp.maximum(last, 0), rows, :], 0.0)

    def piece_sum(p, chunk):
        return tile_sum(0, chunk * 2 + p // 2, pl.ds(p % 2 * PIECE, PIECE))

    def forward_term(p, rows):
        spots = [(lists[0, 2 * p + i], lists[1, 2 * p + i]) for i in range(2)]
        left = jnp.concatenate([narrow[s, rows, :] for s, _ in spots], axis=1)
        right = jnp.concatenate([scaled[c] for _, c in spots], axis=0)
        return jnp.dot(left, right, preferred_element_type=F32)

    x_sends = [group() for _ in range(PIECES)]
    nothing = jnp.zeros((64, T), F32)
    for i in range(2):

        products(0, forward_term, half(i), 0, PAIRS, nothing)

        for p in (i, i + 2):
            for k in NEAR:
                for zc in range(4):
                    part[p, k, zc] = piece_sum(p, x_at[k] * 4 + zc).astype(BF16)
                send(part.at[p, k], x_in.at[k, p], x_to[k], x_sends[p])

    total = row_count[x]
    wait(rx, rx_in)
    for k in range(3):
        total = total + rx_in[k]
    rx_sum[...] = total
    rz = group()
    for k in range(3):
        send(rx_sum, rz_in.at[k], z_to[k], rz)

    def x_total(p):
        wait(x_sends[p], back.at[pl.ds(0, 6)])
        z_sends = group()
        for e in (2, 1, 3, 0):
            zc = z if e == 0 else z_at[e - 1]
            total = piece_sum(p, x * 4 + zc)
            for k in range(3):
                total = total + x_in[k, p, zc].astype(F32)
            if e:
                z_buf[p, e - 1] = total.astype(BF16)
                send(z_buf.at[p, e - 1], z_in.at[p, e - 1], z_to[e - 1], z_sends)
        return total, z_sends

    def activate(p, total, z_sends):
        wait(z_sends, z_in.at[p])
        for k in range(3):
            total = total + z_in[p, k].astype(F32)
        span = pl.ds(p * PIECE, PIECE)
        scale = scales[p // 2][p % 2 * PIECE:p % 2 * PIECE + PIECE]
        pre = scale * split_dot(total, weight[...]) + bias[...]
        sig = jax.nn.sigmoid(pre)
        act_out[span, :] = (pre * sig).astype(BF16)
        grad_pre = cot[span, :].astype(F32) * sig * (1.0 + pre * (1.0 - sig))
        sent = (scale * grad_pre).astype(BF16)
        turned = lax.dot_general(
            weight[...], sent, (((1,), (1,)), ((), ())), preferred_element_type=F32
        )
        back_in[p, col] = jnp.concatenate([turned[:64], turned[64:]], axis=1).astype(BF16)
        mine = back_in.at[p, col]
        for k in (1, 0, 2):
            send(mine, mine, z_to[k], hz[p][k])
        for k in NEAR:
            send(mine, mine, x_to[k], hx[p // 2][3])
        return total, sent, jnp.sum(grad_pre, axis=0, keepdims=True)

    hz = [[group() for _ in range(3)] for _ in range(PIECES)]
    hx = [[group() for _ in range(4)] for _ in range(2)]

    def pass_on(p):
        for k in (0, 2, 1):
            wait(hz[p][k], z_in.at[0, 0])
            block = back_in.at[p, x * 4 + z_from[k]]
            for j in NEAR:
                send(block, block, x_to[j], hx[p // 2][k])

    low = lax.broadcasted_iota(jnp.int32, (64, T), 1) < 64

    def place_back(h):
        for k, zc in ((3, z), (0, z_from[0]), (2, z_from[2]), (1, z_from[1])):
            wait(hx[h][k], back.at[pl.ds(0, 3)])
            for xc in range(4):
                j = xc * 4 + zc
                a, b = back_in[2 * h, j].astype(F32), back_in[2 * h + 1, j].astype(F32)
                back[j * 2 + h, 0:64] = jnp.where(low, a, pltpu.roll(b, 64, 1)).astype(BF16)
                back[j * 2 + h, 64:T] = jnp.where(low, pltpu.roll(a, 64, 1), b).astype(BF16)

    aggs, sents, biases = {}, {}, {}
    sums_x = {}
    sums_x[0] = x_total(0)
    total = rx_sum[...]
    wait(rz, rz_in)
    for k in range(3):
        total = total + rz_in[k]
    row_scale[...] = 1.0 / jnp.sqrt(1.0 + total)
    scales = []
    for h in range(2):
        turned = jnp.transpose(jnp.broadcast_to(row_scale[pl.ds(2 * z + h, 1), :], (T, T)))
        scales.append(jnp.concatenate([turned, turned], axis=1))
    for copy in held_in[3:]:
        copy.wait()

    def act(p):
        aggs[p], sents[p], biases[p] = activate(p, *sums_x[p])

    sums_x[2] = x_total(2)
    act(0)
    sums_x[1] = x_total(1)
    act(2)
    sums_x[3] = x_total(3)
    pass_on(0)
    act(1)
    pass_on(2)
    act(3)
    sent = jnp.concatenate([sents[p] for p in range(PIECES)], axis=0)
    agg = jnp.concatenate([aggs[p] for p in range(PIECES)], axis=0)
    turned = jnp.concatenate([jnp.transpose(agg[:T]), jnp.transpose(agg[T:])], axis=1)
    weight_term = split_dot(turned, sent)
    bias_term = jnp.broadcast_to((biases[0] + biases[1]) + (biases[2] + biases[3]), (8, 256))
    for c in range(2):
        for q in range(8):
            at = (q * 2 + c) * 8
            grads[c, q] = weight_term[at:at + 8]
        grads[c, 8] = bias_term
    gsib = group()
    send(grads.at[1 - core], gsib_in, sibling, gsib)
    pass_on(1)
    wait(gsib, gsib_in)
    for q in range(8):
        gq_buf[q, 0] = grads[core, q] + gsib_in[q]
        gq_buf[q, 1] = grads[core, 8] + gsib_in[8]
    gq_in[here] = gq_buf[here]
    gq = group()
    for k, (dz, dy) in enumerate(ROW_STEPS):
        there = ((zl + dz) % 2) * 4 + (y + dy) % 4
        send(gq_buf.at[there], gq_in.at[here], row_to[k], gq)
    pass_on(3)
    wait(gq, gq_in.at[pl.ds(0, far)])
    total = gq_in[0]
    for q in range(1, 8):
        total = total + gq_in[q]
    gz_buf[z] = total
    gz = group()
    for k in range(3):
        send(gz_buf.at[z], gz_buf.at[z], z_to[k], gz)
    place_back(0)
    place_back(1)

    def backward_term(p, rows):
        spots = [(lists[8, 2 * p + i], lists[9, 2 * p + i]) for i in range(2)]
        left = jnp.concatenate([back[r, rows, :] for _, r in spots], axis=1)
        right = jnp.concatenate([narrow[s] for s, _ in spots], axis=0)
        return jnp.dot(left, right, preferred_element_type=F32)

    near = [group(), group()]
    far_sends = [group(), group()]

    def put_col(i):
        for q in range(8):
            for h in range(2):
                t = q * 4 + (1 - core) * 2 + h
                col_part[i, q, h] = tile_sum(8, t, half(i)).astype(BF16)
        send(col_part.at[i], sib_in.at[i], sibling, near[i])

    def pair_up(i):
        wait(near[i], sib_in.at[i])
        for k, (dz, dy) in enumerate(ROW_STEPS):
            q = ((zl + dz) % 2) * 4 + (y + dy) % 4
            for h in range(2):
                own_part = tile_sum(8, q * 4 + core * 2 + h, half(i))
                pair[i, k, h] = (own_part + sib_in[i, q, h].astype(F32)).astype(BF16)
            send(pair.at[i, k], far_in.at[i, k], row_to[k], far_sends[i])

    products(8, backward_term, half(0), 0, PAIRS, nothing)
    put_col(0)
    acc = products(8, backward_term, half(1), 0, PAIRS // 3, nothing)
    wait(gz, gz_buf.at[pl.ds(0, 3)])
    gx_buf[x] = (gz_buf[0] + gz_buf[1]) + (gz_buf[2] + gz_buf[3])
    gx = group()
    for k in range(3):
        send(gx_buf.at[x], gx_buf.at[x], x_to[k], gx)
    products(8, backward_term, half(1), PAIRS // 3, PAIRS, acc)
    put_col(1)
    pair_up(0)
    wait(gx, gx_buf.at[pl.ds(0, 3)])
    total = ((gx_buf[0] + gx_buf[1]) + (gx_buf[2] + gx_buf[3])) * factor
    gall[here, core] = total[0]
    bias_out[...] = total[1, 0:1]
    mine = gall.at[here, core]
    ga = group()
    for device in row_to:
        send(mine, mine, device, ga)
    pair_up(1)
    blocks = [
        jnp.concatenate(
            [
                tile_sum(8, here * 4 + core * 2 + h, half(i)) + sib_in[i, here, h].astype(F32)
                for i in range(2)
            ],
            axis=0,
        )
        for h in range(2)
    ]
    wait(ga, gall.at[pl.ds(0, far), 0])
    held = gall.at[:, core]
    gs = group()
    send(held, held, sibling, gs)
    for i in range(2):
        wait(far_sends[i], far_in.at[i])
    for k in range(far):
        for h in range(2):
            both = jnp.concatenate([far_in[0, k, h], far_in[1, k, h]], axis=0)
            blocks[h] = blocks[h] + both.astype(F32)
    for h in range(2):
        block = blocks[h] * scale_keep[pl.ds(row * 2 + h, 1), :]
        feat_out[pl.ds(h * T, T), :] = jnp.transpose(block).astype(BF16)
    wait(gs, held)
    weight_out[...] = gall[...]
    links.drain()
    assert links.groups <= GROUPS


def emit_kernel(*refs):
    copies = [pltpu.make_async_copy(refs[k], refs[4 + k], refs[8].at[k]) for k in range(4)]
    for copy in copies:
        copy.start()
    for copy in copies:
        copy.wait()


def on_device(features, weight, bias, cotangent, tile_rows, tile_cols, tile_mask):
    nodes = features.shape[0] * lax.axis_size("row") * lax.axis_size("col")
    anywhere = pl.BlockSpec(memory_space=pl.ANY)
    vmem = pl.BlockSpec(memory_space=pltpu.VMEM)
    dma = pltpu.SemaphoreType.DMA
    shape = jax.ShapeDtypeStruct
    far = len(ROW_STEPS)
    outs = (
        shape((256, 256), BF16),
        shape((256, T), BF16),
        shape((8, 2, 8, 256), F32),
        shape((1, 256), F32),
    )
    results = pl.pallas_call(
        functools.partial(layer_kernel, 1.0 / float(nodes) ** 0.5),
        out_shape=tuple(pltpu.VMEM(out.shape, out.dtype) for out in outs),
        in_specs=[pl.BlockSpec(memory_space=pltpu.HBM)] * 7,
        out_specs=(vmem,) * 4,
        scratch_shapes=[
            pltpu.VMEM((T, 256), BF16),
            pltpu.VMEM((1, 256), F32),
            pltpu.VMEM((256, 256), BF16),
            pltpu.VMEM((1, SLOTS), jnp.int32),
            pltpu.VMEM((1, SLOTS), jnp.int32),
            pltpu.VMEM((SLOTS, T, T), jnp.int32),
            pltpu.VMEM((SLOTS + 1, T, T), BF16),
            pltpu.VMEM((PAIRS, T, T), F32),
            pltpu.VMEM((16, 256), jnp.int32),
            pltpu.VMEM((16, 256), jnp.int32),
            pltpu.SMEM((16, 256), jnp.int32),
            pltpu.VMEM((2, 8, 256, T), BF16),
            pltpu.VMEM((SLOTS, T), F32),
            pltpu.VMEM((32, T), F32),
            pltpu.VMEM((32, T), F32),
            pltpu.VMEM((32, T), F32),
            pltpu.VMEM((32, T), jnp.int16),
            pltpu.VMEM((far, 32, T), jnp.int16),
            pltpu.VMEM((4, 8, T), F32),
            pltpu.VMEM((3, 8, T), F32),
            pltpu.VMEM((8, T), F32),
            pltpu.VMEM((3, 8, T), F32),
            pltpu.VMEM((32, T, T), BF16),
            pltpu.VMEM((PIECES, 3, 4, PIECE, T), BF16),
            pltpu.VMEM((3, PIECES, 4, PIECE, T), BF16),
            pltpu.VMEM((PIECES, 3, PIECE, T), BF16),
            pltpu.VMEM((PIECES, 3, PIECE, T), BF16),
            pltpu.VMEM((PIECES, 16, PIECE, T), BF16),
            pltpu.VMEM((32, T, T), BF16),
            pltpu.VMEM((32, T), F32),
            pltpu.VMEM((8, T), F32),
            pltpu.VMEM((2, 9, 8, 256), F32),
            pltpu.VMEM((9, 8, 256), F32),
            pltpu.VMEM((8, 2, 8, 256), F32),
            pltpu.VMEM((8, 2, 8, 256), F32),
            pltpu.VMEM((4, 2, 8, 256), F32),
            pltpu.VMEM((4, 2, 8, 256), F32),
            pltpu.VMEM((8, 2, 8, 256), F32),
            pltpu.VMEM((2, 8, 2, 64, T), BF16),
            pltpu.VMEM((2, 8, 2, 64, T), BF16),
            pltpu.VMEM((2, far, 2, 64, T), BF16),
            pltpu.VMEM((2, far, 2, 64, T), BF16),
            dma((SLOTS // CHUNK,)),
            dma,
            dma((6,)),
            dma((SENDS,)),
            dma((GROUPS,)),
        ],
        compiler_params=pltpu.CompilerParams(
            vmem_limit_bytes=VMEM_LIMIT, has_side_effects=True, collective_id=1
        ),
        name="layer",
    )(
        features,
        weight,
        bias.reshape(1, 256),
        cotangent,
        tile_rows.reshape(1, SLOTS),
        tile_cols.reshape(1, SLOTS),
        tile_mask.reshape(SLOTS, T, T),
    )
    activations, grad_features, grad_weight, grad_bias = pl.pallas_call(
        emit_kernel,
        out_shape=outs,
        in_specs=[vmem] * 4,
        out_specs=(anywhere,) * 4,
        scratch_shapes=[dma((4,))],
        name="emit",
    )(*(pltpu.with_memory_space_constraint(r, pltpu.VMEM) for r in results))
    return (activations, grad_features, grad_weight.reshape(T, 256), grad_bias.reshape(256))


def solution(mesh):
    placed = (
        P(("col", "row"), None),
        P(),
        P(),
        P(("row", "col"), None),
        P("row", "col", None),
        P("row", "col", None),
        P("row", "col", None, None, None),
    )
    return jax.shard_map(
        on_device,
        mesh=mesh,
        in_specs=placed,
        out_specs=(P(("row", "col"), None), P(("col", "row"), None), P(), P()),
        check_vma=False,
    )
```

```python
import functools

import jax
import jax.numpy as jnp
from jax import lax
from jax.experimental import pallas as pl
from jax.experimental.pallas import tpu as pltpu
from jax.sharding import PartitionSpec as P

F32 = jnp.float32
BF16 = jnp.bfloat16
T = 128
SLOTS = 160
CHUNK = 32
GROUP = 32
PAIRS = (SLOTS + 32) // 2
SENDS = 24
GROUPS = 55
VMEM_LIMIT = 56 * 1024 * 1024
ROW_STEPS = tuple((dz, dy) for dz in (1, 0) for dy in (2, 1, 3, 0) if (dz, dy) != (0, 0))
NEAR = (0, 2, 1)
PIECES = 4
PIECE = 256 // PIECES


class Links:
    def __init__(self, send_sems, recv_sems):
        self.send_sems, self.recv_sems = send_sems, recv_sems
        self.open, self.starts, self.groups = {}, 0, 0

    def group(self):
        self.groups += 1
        return self.groups - 1

    def send(self, src, dst, device, group):
        k = self.starts % SENDS
        self.starts += 1
        if k in self.open:
            self.open[k].wait_send()
        copy = pltpu.make_async_remote_copy(
            src_ref=src,
            dst_ref=dst,
            send_sem=self.send_sems.at[k],
            recv_sem=self.recv_sems.at[group],
            device_id=device,
            device_id_type=pl.DeviceIdType.MESH,
        )
        copy.start()
        self.open[k] = copy

    def wait(self, group, ruler):
        pltpu.make_async_copy(ruler, ruler, self.recv_sems.at[group]).wait()

    def drain(self):
        for copy in self.open.values():
            copy.wait_send()


def split_dot(a, b):
    hi = a.astype(BF16)
    lo = (a - hi.astype(F32)).astype(BF16)
    return jnp.dot(hi, b, preferred_element_type=F32) + jnp.dot(lo, b, preferred_element_type=F32)


def sort_lists(ids, others, lists, at):
    lane = lax.broadcasted_iota(jnp.int32, (1, 256), 1)
    key = (jnp.where(lane < SLOTS, ids, 64) * 256 + lane).astype(F32)
    along = jnp.broadcast_to(key, (256, 256))
    down = jnp.transpose(along)
    wide_lane = lax.broadcasted_iota(jnp.int32, (256, 256), 1).astype(F32)
    id_down = jnp.floor(down * (1.0 / 256.0))
    rank = jnp.sum((along < down).astype(F32), axis=1, keepdims=True)
    held = jnp.sum((id_down == wide_lane).astype(F32), axis=0, keepdims=True)
    odd = held - 2.0 * jnp.floor(held * 0.5)
    below = jnp.sum(jnp.where(wide_lane < id_down, odd, 0.0), axis=1, keepdims=True)
    pos = rank + below
    first = 1.0 - (pos - 2.0 * jnp.floor(pos * 0.5))
    place = jnp.where(id_down < 63.0, (pos == wide_lane).astype(F32), 0.0).astype(BF16)
    row = lax.broadcasted_iota(jnp.int32, (8, 256), 0)
    values = jnp.where(row == 0, lane + 1, jnp.where(row == 1, others, ids))
    moved = jnp.dot(values.astype(F32).astype(BF16), place, preferred_element_type=F32)
    upto = jnp.where(id_down <= wide_lane, first, 0.0)
    last = jnp.sum(upto, axis=0, keepdims=True) - 1.0
    found = jnp.where(row == 3, last, moved).astype(jnp.int32)
    least = jnp.where(row == 3, -1, 0)
    most = jnp.where(row == 0, SLOTS, jnp.where(row == 3, PAIRS - 1, 31))
    lists[pl.ds(at, 8), :] = jnp.minimum(jnp.maximum(found, least), most)


def layer_kernel(
    factor,
    feat, weight_hbm, bias_hbm, cot_hbm, row_hbm, col_hbm, mask,
    act_out, feat_out, weight_out, bias_out,
    weight, bias, cot, row_ids, col_ids,
    mask_in, narrow, running, padded, lists_v, lists,
    feats, sums, count, sib_count, pair_count, pair_send, far_count,
    row_count, rx_in, rx_sum, rz_in, scaled,
    part, x_in, z_buf, z_in, back_in, back,
    scale_keep, row_scale, grads, gsib_in, gq_buf, gq_in, gx_buf, gz_buf, gall,
    col_part, sib_in, pair, far_in,
    mask_sem, list_sem, in_sem, send_sems, recv_sems,
):
    row, col = lax.axis_index("row"), lax.axis_index("col")
    zl, y, core = row // 8, (row // 2) % 4, row % 2
    x, z = col // 4, col % 4
    here = zl * 4 + y
    sibling = (zl * 8 + y * 2 + 1 - core, col)
    row_to = [(((zl + dz) % 2) * 8 + ((y + dy) % 4) * 2 + core, col) for dz, dy in ROW_STEPS]
    row_from = [((zl - dz + 2) % 2) * 4 + (y - dy + 4) % 4 for dz, dy in ROW_STEPS]
    far = len(ROW_STEPS)
    x_at = [(x + d) % 4 for d in (1, 2, 3)]
    z_at = [(z + d) % 4 for d in (1, 2, 3)]
    x_to = [(row, p * 4 + z) for p in x_at]
    z_to = [(row, x * 4 + p) for p in z_at]
    x_from = [(x - d + 4) % 4 for d in (1, 2, 3)]
    z_from = [(z - d + 4) % 4 for d in (1, 2, 3)]
    links = Links(send_sems, recv_sems)
    send, wait, group = links.send, links.wait, links.group

    barrier = pltpu.get_barrier_semaphore()
    peers = [sibling] + row_to + x_to + z_to
    for device in peers:
        pl.semaphore_signal(
            barrier, inc=1, device_id=device, device_id_type=pl.DeviceIdType.MESH
        )
    chunks = SLOTS // CHUNK
    loads = []
    held_in = []
    for k, (src, dst) in enumerate(
        (
            (row_hbm, row_ids),
            (col_hbm, col_ids),
            (feat, feats.at[core, here]),
            (weight_hbm, weight),
            (bias_hbm, bias),
            (cot_hbm, cot),
        )
    ):
        held_in.append(pltpu.make_async_copy(src, dst, in_sem.at[k]))
    for copy in held_in[:2]:
        copy.start()
    for c in range(chunks):
        span = pl.ds(c * CHUNK, CHUNK)
        load = pltpu.make_async_copy(mask.at[span], mask_in.at[span], mask_sem.at[c])
        load.start()
        loads.append(load)
        if c == 1:
            for copy in held_in[2:]:
                copy.start()

    narrow[0] = jnp.zeros((T, T), BF16)

    def take(c):
        loads[c].wait()

        def eight(g, carry):
            at = pl.multiple_of(c * CHUNK + g * 8, 8)
            wide = mask_in[pl.ds(at, 8)].astype(F32)
            narrow[pl.ds(at + 1, 8)] = wide.astype(BF16)
            sums[pl.ds(at, 8), :] = jnp.sum(wide, axis=1)
            return carry

        lax.fori_loop(0, CHUNK // 8, eight, 0)

    for c in range(chunks // 2 + 1):
        take(c)
    pl.semaphore_wait(barrier, len(peers))
    held_in[2].wait()
    mine = feats.at[core, here]
    own = [group() for _ in range(far + 1)]
    for k in (0, 1, 2, 3, 4, far):
        send(mine, mine, (row_to + [sibling])[k], own[k])
    for c in range(chunks // 2 + 1, chunks):
        take(c)
    slot_row = lax.broadcasted_iota(jnp.int32, (32, SLOTS), 0)
    for copy in held_in[:2]:
        copy.wait()
    onehot = (slot_row == col_ids[...]).astype(BF16)
    count[...] = jnp.dot(onehot, sums[...].astype(BF16), preferred_element_type=F32)
    near_count = group()
    send(count, sib_count, sibling, near_count)

    wait(near_count, sib_count)
    pair_count[...] = count[...] + sib_count[...]
    pair_send[...] = (pair_count[...].astype(jnp.int32) - SLOTS * T).astype(jnp.int16)
    far_counts = group()
    for k in range(far):
        send(pair_send, far_count.at[k], row_to[k], far_counts)
    for k in (5, 6):
        send(mine, mine, row_to[k], own[k])
    padded[...] = jnp.zeros_like(padded)
    padded[0:1, 0:SLOTS] = row_ids[...]
    padded[8:9, 0:SLOTS] = col_ids[...]
    rows_wide, cols_wide = padded[0:1, :], padded[8:9, :]
    sort_lists(rows_wide, cols_wide, lists_v, 0)
    sort_lists(cols_wide, rows_wide, lists_v, 8)
    list_copy = pltpu.make_async_copy(lists_v, lists, list_sem)
    list_copy.start()
    ones = jnp.ones((8, T), BF16)

    def row_sums(g, carry):
        at = pl.multiple_of(g * 8, 8)
        tiles = narrow[pl.ds(at + 1, 8)].reshape(8 * T, T)
        got = lax.dot_general(ones, tiles, (((1,), (1,)), ((), ())), preferred_element_type=F32)
        sums[pl.ds(at, 8), :] = jnp.concatenate(
            [got[0:1, i * T:(i + 1) * T] for i in range(8)], axis=0
        )
        return carry

    lax.fori_loop(0, SLOTS // 8, row_sums, 0)
    onehot = (slot_row == row_ids[...]).astype(BF16)
    got = jnp.dot(onehot, sums[...].astype(BF16), preferred_element_type=F32)
    for c in range(4):
        row_count[c] = got[c * 8:c * 8 + 8]
    rx = group()
    for k in range(3):
        send(row_count.at[x_at[k]], rx_in.at[k], x_to[k], rx)
    forwards = [group(), group()]

    def forward_block(k):
        wait(own[k], feats.at[0, 0])
        block = feats.at[core, row_from[k]]
        send(block, block, sibling, forwards[k // 5])

    for k in range(5):
        forward_block(k)
    total = pair_count[...]
    wait(far_counts, far_count)
    for k in range(far):
        total = total + (far_count[k].astype(jnp.int32) + SLOTS * T).astype(F32)
    scale_keep[...] = 1.0 / jnp.sqrt(1.0 + total)
    order = row_from + [here]
    parts = [scale_keep[pl.ds((q * 2 + c) * 2, 2), :] for c in (core, 1 - core) for q in order]
    turned = jnp.transpose(jnp.concatenate(parts + [jnp.zeros((96, T), F32)], axis=0))

    def scale_block(side, k):
        c, q = (core, 1 - core)[side], order[k]
        for h in range(2):
            lane = side * 16 + k * 2 + h
            block = feats[c, q, pl.ds(h * T, T), :].astype(F32)
            scaled[(q * 2 + c) * 2 + h] = (block * turned[:, lane:lane + 1]).astype(BF16)

    for k in (far, 0, 1, 2, 3, 4):
        scale_block(0, k)
    for k in (5, 6):
        forward_block(k)
    scale_block(0, 5)
    scale_block(0, 6)
    wait(own[far], feats.at[0, 0])
    scale_block(1, far)
    wait(forwards[0], feats.at[0, pl.ds(0, 5)])
    for k in range(5):
        scale_block(1, k)
    wait(forwards[1], feats.at[0, pl.ds(0, 2)])
    scale_block(1, 5)
    scale_block(1, 6)
    list_copy.wait()

    def half(i):
        return pl.ds(i * 64, 64)

    def products(at, term, rows, begin, end, acc, size=PAIRS // 2):
        def group_of(g, acc):
            terms = [term(g * size + i, rows) for i in range(size)]
            for i in range(size):
                p = g * size + i
                same = lists[at + 2, 2 * p] == lists[at + 2, 2 * jnp.maximum(p - 1, 0)]
                acc = jnp.where(same, acc, 0.0) + terms[i]
                running[p, rows, :] = acc
            return acc

        return lax.fori_loop(begin // size, end // size, group_of, acc)

    def tile_sum(at, t, rows=pl.ds(0, T)):
        last = lists[at + 3, t]
        before = jnp.where(t > 0, lists[at + 3, jnp.maximum(t - 1, 0)], -1)
        return jnp.where(last > before, running[jnp.maximum(last, 0), rows, :], 0.0)

    def piece_sum(p, chunk):
        return tile_sum(0, chunk * 2 + p // 2, pl.ds(p % 2 * PIECE, PIECE))

    def forward_term(p, rows):
        spots = [(lists[0, 2 * p + i], lists[1, 2 * p + i]) for i in range(2)]
        left = jnp.concatenate([narrow[s, rows, :] for s, _ in spots], axis=1)
        right = jnp.concatenate([scaled[c] for _, c in spots], axis=0)
        return jnp.dot(left, right, preferred_element_type=F32)

    x_sends = [group() for _ in range(PIECES)]
    nothing = jnp.zeros((64, T), F32)
    for i in range(2):

        products(0, forward_term, half(i), 0, PAIRS, nothing)

        for p in (i, i + 2):
            for k in NEAR:
                for zc in range(4):
                    part[p, k, zc] = piece_sum(p, x_at[k] * 4 + zc).astype(BF16)
                send(part.at[p, k], x_in.at[k, p], x_to[k], x_sends[p])

    total = row_count[x]
    wait(rx, rx_in)
    for k in range(3):
        total = total + rx_in[k]
    rx_sum[...] = total
    rz = group()
    for k in range(3):
        send(rx_sum, rz_in.at[k], z_to[k], rz)

    def x_total(p):
        wait(x_sends[p], back.at[pl.ds(0, 6)])
        z_sends = group()
        for e in (2, 1, 3, 0):
            zc = z if e == 0 else z_at[e - 1]
            total = piece_sum(p, x * 4 + zc)
            for k in range(3):
                total = total + x_in[k, p, zc].astype(F32)
            if e:
                z_buf[p, e - 1] = total.astype(BF16)
                send(z_buf.at[p, e - 1], z_in.at[p, e - 1], z_to[e - 1], z_sends)
        return total, z_sends

    def activate(p, total, z_sends):
        wait(z_sends, z_in.at[p])
        for k in range(3):
            total = total + z_in[p, k].astype(F32)
        span = pl.ds(p * PIECE, PIECE)
        scale = scales[p // 2][p % 2 * PIECE:p % 2 * PIECE + PIECE]
        pre = scale * split_dot(total, weight[...]) + bias[...]
        sig = jax.nn.sigmoid(pre)
        act_out[span, :] = (pre * sig).astype(BF16)
        grad_pre = cot[span, :].astype(F32) * sig * (1.0 + pre * (1.0 - sig))
        sent = (scale * grad_pre).astype(BF16)
        turned = lax.dot_general(
            weight[...], sent, (((1,), (1,)), ((), ())), preferred_element_type=F32
        )
        back_in[p, col] = jnp.concatenate([turned[:64], turned[64:]], axis=1).astype(BF16)
        mine = back_in.at[p, col]
        for k in (1, 0, 2):
            send(mine, mine, z_to[k], hz[p][k])
        for k in NEAR:
            send(mine, mine, x_to[k], hx[p // 2][3])
        return total, sent, jnp.sum(grad_pre, axis=0, keepdims=True)

    hz = [[group() for _ in range(3)] for _ in range(PIECES)]
    hx = [[group() for _ in range(4)] for _ in range(2)]

    def pass_on(p):
        for k in (0, 2, 1):
            wait(hz[p][k], z_in.at[0, 0])
            block = back_in.at[p, x * 4 + z_from[k]]
            for j in NEAR:
                send(block, block, x_to[j], hx[p // 2][k])

    low = lax.broadcasted_iota(jnp.int32, (64, T), 1) < 64

    def place_back(h):
        for k, zc in ((3, z), (0, z_from[0]), (2, z_from[2]), (1, z_from[1])):
            wait(hx[h][k], back.at[pl.ds(0, 3)])
            for xc in range(4):
                j = xc * 4 + zc
                a, b = back_in[2 * h, j].astype(F32), back_in[2 * h + 1, j].astype(F32)
                back[j * 2 + h, 0:64] = jnp.where(low, a, pltpu.roll(b, 64, 1)).astype(BF16)
                back[j * 2 + h, 64:T] = jnp.where(low, pltpu.roll(a, 64, 1), b).astype(BF16)

    aggs, sents, biases = {}, {}, {}
    sums_x = {}
    sums_x[0] = x_total(0)
    total = rx_sum[...]
    wait(rz, rz_in)
    for k in range(3):
        total = total + rz_in[k]
    row_scale[...] = 1.0 / jnp.sqrt(1.0 + total)
    scales = []
    for h in range(2):
        turned = jnp.transpose(jnp.broadcast_to(row_scale[pl.ds(2 * z + h, 1), :], (T, T)))
        scales.append(jnp.concatenate([turned, turned], axis=1))
    for copy in held_in[3:]:
        copy.wait()

    def act(p):
        aggs[p], sents[p], biases[p] = activate(p, *sums_x[p])

    sums_x[2] = x_total(2)
    act(0)
    sums_x[1] = x_total(1)
    act(2)
    sums_x[3] = x_total(3)
    pass_on(0)
    act(1)
    pass_on(2)
    act(3)
    sent = jnp.concatenate([sents[p] for p in range(PIECES)], axis=0)
    agg = jnp.concatenate([aggs[p] for p in range(PIECES)], axis=0)
    turned = jnp.concatenate([jnp.transpose(agg[:T]), jnp.transpose(agg[T:])], axis=1)
    weight_term = split_dot(turned, sent)
    bias_term = jnp.broadcast_to((biases[0] + biases[1]) + (biases[2] + biases[3]), (8, 256))
    for c in range(2):
        for q in range(8):
            at = (q * 2 + c) * 8
            grads[c, q] = weight_term[at:at + 8]
        grads[c, 8] = bias_term
    gsib = group()
    send(grads.at[1 - core], gsib_in, sibling, gsib)
    pass_on(1)
    wait(gsib, gsib_in)
    for q in range(8):
        gq_buf[q, 0] = grads[core, q] + gsib_in[q]
        gq_buf[q, 1] = grads[core, 8] + gsib_in[8]
    gq_in[here] = gq_buf[here]
    gq = group()
    for k, (dz, dy) in enumerate(ROW_STEPS):
        there = ((zl + dz) % 2) * 4 + (y + dy) % 4
        send(gq_buf.at[there], gq_in.at[here], row_to[k], gq)
    pass_on(3)
    wait(gq, gq_in.at[pl.ds(0, far)])
    total = gq_in[0]
    for q in range(1, 8):
        total = total + gq_in[q]
    gz_buf[z] = total
    gz = group()
    for k in range(3):
        send(gz_buf.at[z], gz_buf.at[z], z_to[k], gz)
    place_back(0)
    place_back(1)

    def backward_term(p, rows):
        spots = [(lists[8, 2 * p + i], lists[9, 2 * p + i]) for i in range(2)]
        left = jnp.concatenate([back[r, rows, :] for _, r in spots], axis=1)
        right = jnp.concatenate([narrow[s] for s, _ in spots], axis=0)
        return jnp.dot(left, right, preferred_element_type=F32)

    near = [group(), group()]
    far_sends = [group(), group()]

    def put_col(i):
        for q in range(8):
            for h in range(2):
                t = q * 4 + (1 - core) * 2 + h
                col_part[i, q, h] = tile_sum(8, t, half(i)).astype(BF16)
        send(col_part.at[i], sib_in.at[i], sibling, near[i])

    def pair_up(i):
        wait(near[i], sib_in.at[i])
        for k, (dz, dy) in enumerate(ROW_STEPS):
            q = ((zl + dz) % 2) * 4 + (y + dy) % 4
            for h in range(2):
                own_part = tile_sum(8, q * 4 + core * 2 + h, half(i))
                pair[i, k, h] = (own_part + sib_in[i, q, h].astype(F32)).astype(BF16)
            send(pair.at[i, k], far_in.at[i, k], row_to[k], far_sends[i])

    products(8, backward_term, half(0), 0, PAIRS, nothing)
    put_col(0)
    acc = products(8, backward_term, half(1), 0, PAIRS // 3, nothing, GROUP)
    wait(gz, gz_buf.at[pl.ds(0, 3)])
    gx_buf[x] = (gz_buf[0] + gz_buf[1]) + (gz_buf[2] + gz_buf[3])
    gx = group()
    for k in range(3):
        send(gx_buf.at[x], gx_buf.at[x], x_to[k], gx)
    products(8, backward_term, half(1), PAIRS // 3, PAIRS, acc, GROUP)
    put_col(1)
    pair_up(0)
    wait(gx, gx_buf.at[pl.ds(0, 3)])
    total = ((gx_buf[0] + gx_buf[1]) + (gx_buf[2] + gx_buf[3])) * factor
    gall[here, core] = total[0]
    bias_out[...] = total[1, 0:1]
    mine = gall.at[here, core]
    ga = group()
    for device in row_to:
        send(mine, mine, device, ga)
    pair_up(1)
    blocks = [
        jnp.concatenate(
            [
                tile_sum(8, here * 4 + core * 2 + h, half(i)) + sib_in[i, here, h].astype(F32)
                for i in range(2)
            ],
            axis=0,
        )
        for h in range(2)
    ]
    wait(ga, gall.at[pl.ds(0, far), 0])
    held = gall.at[:, core]
    gs = group()
    send(held, held, sibling, gs)
    for i in range(2):
        wait(far_sends[i], far_in.at[i])
    for k in range(far):
        for h in range(2):
            both = jnp.concatenate([far_in[0, k, h], far_in[1, k, h]], axis=0)
            blocks[h] = blocks[h] + both.astype(F32)
    for h in range(2):
        block = blocks[h] * scale_keep[pl.ds(row * 2 + h, 1), :]
        feat_out[pl.ds(h * T, T), :] = jnp.transpose(block).astype(BF16)
    wait(gs, held)
    weight_out[...] = gall[...]
    links.drain()
    assert links.groups <= GROUPS


def emit_kernel(*refs):
    copies = [pltpu.make_async_copy(refs[k], refs[4 + k], refs[8].at[k]) for k in range(4)]
    for copy in copies:
        copy.start()
    for copy in copies:
        copy.wait()


def on_device(features, weight, bias, cotangent, tile_rows, tile_cols, tile_mask):
    nodes = features.shape[0] * lax.axis_size("row") * lax.axis_size("col")
    anywhere = pl.BlockSpec(memory_space=pl.ANY)
    vmem = pl.BlockSpec(memory_space=pltpu.VMEM)
    dma = pltpu.SemaphoreType.DMA
    shape = jax.ShapeDtypeStruct
    far = len(ROW_STEPS)
    outs = (
        shape((256, 256), BF16),
        shape((256, T), BF16),
        shape((8, 2, 8, 256), F32),
        shape((1, 256), F32),
    )
    results = pl.pallas_call(
        functools.partial(layer_kernel, 1.0 / float(nodes) ** 0.5),
        out_shape=tuple(pltpu.VMEM(out.shape, out.dtype) for out in outs),
        in_specs=[pl.BlockSpec(memory_space=pltpu.HBM)] * 7,
        out_specs=(vmem,) * 4,
        scratch_shapes=[
            pltpu.VMEM((T, 256), BF16),
            pltpu.VMEM((1, 256), F32),
            pltpu.VMEM((256, 256), BF16),
            pltpu.VMEM((1, SLOTS), jnp.int32),
            pltpu.VMEM((1, SLOTS), jnp.int32),
            pltpu.VMEM((SLOTS, T, T), jnp.int32),
            pltpu.VMEM((SLOTS + 1, T, T), BF16),
            pltpu.VMEM((PAIRS, T, T), F32),
            pltpu.VMEM((16, 256), jnp.int32),
            pltpu.VMEM((16, 256), jnp.int32),
            pltpu.SMEM((16, 256), jnp.int32),
            pltpu.VMEM((2, 8, 256, T), BF16),
            pltpu.VMEM((SLOTS, T), F32),
            pltpu.VMEM((32, T), F32),
            pltpu.VMEM((32, T), F32),
            pltpu.VMEM((32, T), F32),
            pltpu.VMEM((32, T), jnp.int16),
            pltpu.VMEM((far, 32, T), jnp.int16),
            pltpu.VMEM((4, 8, T), F32),
            pltpu.VMEM((3, 8, T), F32),
            pltpu.VMEM((8, T), F32),
            pltpu.VMEM((3, 8, T), F32),
            pltpu.VMEM((32, T, T), BF16),
            pltpu.VMEM((PIECES, 3, 4, PIECE, T), BF16),
            pltpu.VMEM((3, PIECES, 4, PIECE, T), BF16),
            pltpu.VMEM((PIECES, 3, PIECE, T), BF16),
            pltpu.VMEM((PIECES, 3, PIECE, T), BF16),
            pltpu.VMEM((PIECES, 16, PIECE, T), BF16),
            pltpu.VMEM((32, T, T), BF16),
            pltpu.VMEM((32, T), F32),
            pltpu.VMEM((8, T), F32),
            pltpu.VMEM((2, 9, 8, 256), F32),
            pltpu.VMEM((9, 8, 256), F32),
            pltpu.VMEM((8, 2, 8, 256), F32),
            pltpu.VMEM((8, 2, 8, 256), F32),
            pltpu.VMEM((4, 2, 8, 256), F32),
            pltpu.VMEM((4, 2, 8, 256), F32),
            pltpu.VMEM((8, 2, 8, 256), F32),
            pltpu.VMEM((2, 8, 2, 64, T), BF16),
            pltpu.VMEM((2, 8, 2, 64, T), BF16),
            pltpu.VMEM((2, far, 2, 64, T), BF16),
            pltpu.VMEM((2, far, 2, 64, T), BF16),
            dma((SLOTS // CHUNK,)),
            dma,
            dma((6,)),
            dma((SENDS,)),
            dma((GROUPS,)),
        ],
        compiler_params=pltpu.CompilerParams(
            vmem_limit_bytes=VMEM_LIMIT, has_side_effects=True, collective_id=1
        ),
        name="layer",
    )(
        features,
        weight,
        bias.reshape(1, 256),
        cotangent,
        tile_rows.reshape(1, SLOTS),
        tile_cols.reshape(1, SLOTS),
        tile_mask.reshape(SLOTS, T, T),
    )
    activations, grad_features, grad_weight, grad_bias = pl.pallas_call(
        emit_kernel,
        out_shape=outs,
        in_specs=[vmem] * 4,
        out_specs=(anywhere,) * 4,
        scratch_shapes=[dma((4,))],
        name="emit",
    )(*(pltpu.with_memory_space_constraint(r, pltpu.VMEM) for r in results))
    return (activations, grad_features, grad_weight.reshape(T, 256), grad_bias.reshape(256))


def solution(mesh):
    placed = (
        P(("col", "row"), None),
        P(),
        P(),
        P(("row", "col"), None),
        P("row", "col", None),
        P("row", "col", None),
        P("row", "col", None, None, None),
    )
    return jax.shard_map(
        on_device,
        mesh=mesh,
        in_specs=placed,
        out_specs=(P(("row", "col"), None), P(("col", "row"), None), P(), P()),
        check_vma=False,
    )
```
